32 devices in a mesh: gx: 8 (over y, x, core), gy: 4 (over z).
Axes of the slice: x: 2, y: 2, z: 4, core: 2. Of those that a mesh axis runs over, the one named last changes fastest.
Arguments:
- tokens: bfloat16 [8192, 1536], P('gx', 'gy'), may hold values from -6 to 6
- first_gain: float32 [1536], P('gy'), may hold values from 0.5 to 1.5
- w_query: float32 [1536, 1536], P('gx', 'gy'), may hold values from -0.15625 to 0.15625
- w_key: float32 [1536, 512], P('gx', 'gy'), may hold values from -0.15625 to 0.15625
- w_value: float32 [1536, 512], P('gx', 'gy'), may hold values from -0.15625 to 0.15625
- w_out: float32 [1536, 1536], P('gx', 'gy'), may hold values from -0.625 to 0.625
- second_gain: float32 [1536], P('gy'), may hold values from 0.5 to 1.5
- w_router: float32 [1536, 40], P('gx'), may hold values from -0.078125 to 0.078125
- w_gate: float32 [1536, 40, 512], P('gx', None, 'gy'), may hold values from -0.15625 to 0.15625
- w_up: float32 [1536, 40, 512], P('gx', None, 'gy'), may hold values from -0.15625 to 0.15625
- w_down: float32 [1536, 40, 512], P('gx', None, 'gy'), may hold values from -0.75 to 0.75
- routes: int32 [8192, 8], P('gx'), may hold values from 0 to 39, all different within a row; in each aligned block of 1024 rows (0 to 1023, 1024 to 2047, ...) at most 256 rows name the same one
- block_cotangent: bfloat16 [8192, 1536], P('gx', 'gy'), may hold values from -6 to 6
Outputs:
- block_out: bfloat16 [8192, 1536], P('gx', 'gy')
- input_grad: bfloat16 [8192, 1536], P('gx', 'gy')
- first_gain_grad: float32 [1536], P('gy')
- query_grad: float32 [1536, 1536], P('gx', 'gy')
- key_grad: float32 [1536, 512], P('gx', 'gy')
- value_grad: float32 [1536, 512], P('gx', 'gy')
- out_proj_grad: float32 [1536, 1536], P('gx', 'gy')
- second_gain_grad: float32 [1536], P('gy')
- router_grad: float32 [1536, 40], P('gx')
- gate_grad: float32 [1536, 40, 512], P('gx', None, 'gy')
- up_grad: float32 [1536, 40, 512], P('gx', None, 'gy')
- down_grad: float32 [1536, 40, 512], P('gx', None, 'gy')
The draws below stay inside these ranges and needn't reach their ends.
Inputs may be any that keep to these rules, and one draw needn't show every extreme that they name: `routes`: each row names 8 different experts. Within the rows of one device (aligned blocks of 1024 rows) no expert is named by more than 256 rows, and in every draw some expert is named by exactly 256 rows of some block.
All inputs are finite; a program needn't handle non-finite values.
Results may differ from the reference program's by a relative error of at most 0.018.
Values may be sent and summed in bfloat16 or wider, within the bound.
No kernel may reach another device: no remote copies, remote signals or barrier semaphores. Data moves between devices by JAX's collectives and lax.ppermute only.
A program may use at most 448 MiB of HBM per device.

```python
import math
import jax
import jax.numpy as jnp
import numpy as np
from jax import lax

D = 1536
H = 24
KV = 8
HD = 64
FF = 512
EXPERTS = 40
TOP = 8
TOK_DEV = 1024
CAP = 256
TOKENS = 8192
N_GX = 8


def raised(entries, key, source, target, shards_of, factor):
    owner, partner = [(jnp.arange(entries.shape[position]) // (entries.shape[position] // shards_of)).reshape([-1 if axis == position else 1 for axis in range(entries.ndim)]) for position in (source, target)]
    chosen = jax.random.permutation(key, shards_of)[partner]
    strong = (owner == chosen) | (owner == (partner + shards_of // 2) % shards_of)
    return jnp.where(strong, factor * entries, entries)


def block_levels(key, extent, pieces, low, high):
    level = 1.0
    for position, blocks in pieces:
        heights = jax.random.uniform(jax.random.fold_in(jax.random.fold_in(key, 6), position), (blocks,), jnp.float32, low / len(pieces), high / len(pieces))
        level = level * jnp.repeat(jnp.exp(heights), extent[position] // blocks).reshape((-1,) + (1,) * (len(extent) - 1 - position))
    return level


def assign_block(own_key, own, number, rows, number_of, top, most, slope):
    order = jax.random.permutation(own_key, number_of)
    packed, usual = load_shares(number_of, rows * top, most, slope, True), load_shares(number_of, rows * top, most, slope, False)
    places = jnp.arange(number_of)

    def named(sizes, rotation):
        used = int((sizes > 0).sum())
        fixed = max(1, used // 4)
        shifted = fixed + (places - fixed + rotation * (used - fixed)) % max(1, number_of - fixed)
        return jnp.zeros((number_of,), jnp.int32).at[order[jnp.where(places < fixed, places, shifted)]].set(jnp.asarray(sizes, jnp.int32))

    sizes = jnp.where(number % 4 == 0, named(packed, number // 4), named(usual, number - number // 4 - 1))
    mixed = jax.random.permutation(jax.random.fold_in(own, 3), number_of)
    donor, taker = mixed[0:number_of // 2 * 2:2], mixed[1:number_of // 2 * 2:2]
    margin = jnp.minimum(sizes[donor] - 1, most - sizes[taker]) // 2
    margin = jnp.where((donor == order[0]) | (taker == order[0]) | (sizes[taker] == 0), 0, jnp.maximum(margin, 0))
    shifted = jax.random.randint(jax.random.fold_in(own, 4), (number_of // 2,), 0, 1 << 20) % (margin + 1)
    sizes = sizes.at[donor].add(-shifted).at[taker].add(shifted)
    items = jnp.searchsorted(jnp.cumsum(sizes), jnp.arange(rows * top), side="right").astype(jnp.int32)
    listing = items.reshape(top, rows).T
    listing = listing[jax.random.permutation(jax.random.fold_in(own, 1), rows)]
    rotation = jax.random.randint(jax.random.fold_in(own, 2), (rows, 1), 0, top)
    return jnp.take_along_axis(listing, (jnp.arange(top)[None, :] + rotation) % top, axis=1)


def load_shares(count, total, bound, skew, full):
    loads = [(1 << 20) // math.isqrt(standing ** skew) + 1 for standing in range(1, count + 1)]
    largest = bound if full else min(bound, max(-(-total // count), total * loads[0] // sum(loads)))
    least = 1 if total - largest >= count - 1 else 0
    counts, rest = [largest] + [least] * (count - 1), total - largest - least * (count - 1)
    while rest > 0:
        free = [i for i in range(1, count) if counts[i] < largest] or [i for i in range(1, count) if counts[i] < bound]
        mass, budget = sum([loads[i] for i in free]), rest
        for i in free:
            extra = min(bound - counts[i], max(1, budget * loads[i] // mass), rest)
            counts[i] = counts[i] + extra
            rest = rest - extra
    return np.array(counts)


def scatter_about(own_key, shape, width, reach, shards=(), held_as=jnp.bfloat16):
    gain = block_levels(own_key, shape, shards, -0.22, 0.18) if shards else 1.0
    drawn = jax.random.normal(own_key, shape, jnp.float32) * width * gain
    return jnp.minimum(jnp.maximum(drawn, -reach), reach).astype(held_as)


def noise_with(own_key, extent, scale, most, cuts, heavy, kind=jnp.bfloat16):
    array = scale * jax.random.normal(own_key, extent, jnp.float32)
    if cuts:
        array = array * block_levels(own_key, extent, cuts, -0.22, 0.18)
    return jnp.clip(raised(array, jax.random.fold_in(own_key, 3), *heavy), -most, most).astype(kind)


def setup_inputs(seed: int = 0) -> dict:
    arg_keys = jax.random.split(jax.random.key(seed), 14)
    tokens = noise_with(arg_keys[0], (TOKENS, D), 1.0, 6.0, ((0, 8), (1, 4)), (0, 1, 8, 2.0))
    first_gain = jnp.clip(1.0 + 0.1 * jax.random.normal(arg_keys[1], (D,), jnp.float32), 0.5, 1.5)
    w_query = scatter_about(arg_keys[2], (D, H * HD), D ** -0.5, 0.15625, ((0, 8), (1, 4)), jnp.float32)
    w_key = scatter_about(arg_keys[3], (D, KV * HD), D ** -0.5, 0.15625, ((0, 8), (1, 4)), jnp.float32)
    w_value = scatter_about(arg_keys[4], (D, KV * HD), D ** -0.5, 0.15625, ((0, 8), (1, 4)), jnp.float32)
    w_out = scatter_about(arg_keys[5], (D, H * HD), (H * HD // 16) ** -0.5, 0.625, ((0, 8), (1, 4)), jnp.float32)
    second_gain = jnp.clip(1.0 + 0.1 * jax.random.normal(arg_keys[6], (D,), jnp.float32), 0.5, 1.5)
    w_router = scatter_about(arg_keys[7], (D, EXPERTS), (4 * D) ** -0.5, 0.078125, ((0, 8),), jnp.float32)
    w_gate = scatter_about(arg_keys[8], (D, EXPERTS, FF), D ** -0.5, 0.15625, ((0, 8), (2, 4)), jnp.float32)
    w_up = scatter_about(arg_keys[9], (D, EXPERTS, FF), D ** -0.5, 0.15625, ((0, 8), (2, 4)), jnp.float32)
    w_down = scatter_about(arg_keys[10], (D, EXPERTS, FF), (FF // 8) ** -0.5, 0.75, ((0, 8), (2, 4)), jnp.float32)
    routes_keys = jax.random.split(jax.random.fold_in(arg_keys[11], 1), TOKENS // TOK_DEV)
    routes_turns = jax.random.permutation(jax.random.fold_in(arg_keys[11], 3), TOKENS // TOK_DEV)
    routes = jax.vmap(lambda own, number: assign_block(jax.random.fold_in(arg_keys[11], 2), own, number, TOK_DEV, EXPERTS, TOP, CAP, 1))(routes_keys, routes_turns).reshape((TOKENS, TOP))
    block_cotangent = noise_with(arg_keys[12], (TOKENS, D), 1.0, 6.0, ((0, 8), (1, 4)), (0, 1, 8, 2.0))
    return dict(tokens=tokens, first_gain=first_gain, w_query=w_query, w_key=w_key, w_value=w_value, w_out=w_out, second_gain=second_gain, w_router=w_router, w_gate=w_gate, w_up=w_up, w_down=w_down, routes=routes, block_cotangent=block_cotangent)


highest = lax.Precision.HIGHEST

@jax.custom_vjp
def low(v):
    return lax.optimization_barrier(v.astype(jnp.bfloat16)).astype(jnp.float32)

@jax.custom_vjp
def low_back(v):
    return v

def low_keep(v):
    return (low(v), None)

def low_pass(kept, grad):
    return (grad,)

def back_keep(v):
    return (v, None)

def back_low(kept, grad):
    return (low(grad),)
low.defvjp(low_keep, low_pass)
low_back.defvjp(back_keep, back_low)

def rms_scale(values):
    return lax.rsqrt(lax.optimization_barrier(jnp.mean(values * values, axis=-1, keepdims=True)) + 1e-06)

def rope_tables(positions):
    half_width = HD // 2
    frequency = jnp.exp(jnp.arange(half_width, dtype=jnp.float32) * (-2.0 * math.log(10000.0) / HD))
    angles = positions[:, None] * frequency[None, :]
    return (jnp.cos(angles)[:, None, :], jnp.sin(angles)[:, None, :])

def rotate(values, cosine, sine_tab):
    half_width = values.shape[-1] // 2
    first_half = values[..., :half_width]
    second_half = values[..., half_width:]
    return jnp.concatenate([first_half * cosine - second_half * sine_tab, second_half * cosine + first_half * sine_tab], axis=-1)

def attend_one(batch_items):
    query_rows, key_rows, value_rows = batch_items
    groups = query_rows.shape[1] // key_rows.shape[1]
    key_rows = jnp.repeat(key_rows, groups, axis=1)
    value_rows = jnp.repeat(value_rows, groups, axis=1)
    scores = low_back(jnp.einsum('qhd,khd->hqk', query_rows, key_rows, precision=highest) * HD ** (-0.5))
    length = query_rows.shape[0]
    causal = jnp.arange(length)[:, None] >= jnp.arange(length)[None, :]
    scores = jnp.where(causal[None], scores, -1e+30)
    attn_probs = jax.nn.softmax(scores, axis=-1)
    return jnp.einsum('hqk,khd->qhd', low(attn_probs), value_rows, precision=highest)

def mix_one(normed, gate_probs, route_rows, gate_w, up_w, down_w):
    length = normed.shape[0]
    chosen_hot = (route_rows[:, :, None] == jnp.arange(EXPERTS, dtype=jnp.int32)[None, None, :]).astype(jnp.int32)
    member = lax.optimization_barrier(jnp.sum(chosen_hot, axis=1))
    before = jnp.cumsum(member, axis=0) - member
    slot_rank = jnp.take_along_axis(before, route_rows, axis=1).astype(jnp.int32)
    token_ids = jnp.broadcast_to(jnp.arange(length, dtype=jnp.int32)[:, None], route_rows.shape)
    slot_owner = jnp.full((EXPERTS, CAP), length, jnp.int32).at[route_rows, slot_rank].set(token_ids)
    slot_share = jnp.zeros((EXPERTS, CAP), jnp.float32).at[route_rows, slot_rank].set(gate_probs)
    padded = jnp.concatenate([normed, jnp.zeros((1, normed.shape[1]), jnp.float32)], axis=0)
    slot_rows = padded[slot_owner]
    gate_pre = low_back(jnp.einsum('ecd,def->ecf', slot_rows, gate_w, precision=highest))
    up_pre = low_back(jnp.einsum('ecd,def->ecf', slot_rows, up_w, precision=highest))
    active = low(jax.nn.silu(gate_pre) * up_pre)
    expert_y = low_back(jnp.einsum('ecf,def->ecd', active, down_w, precision=highest))
    summed = jnp.zeros((length + 1, normed.shape[1]), jnp.float32).at[slot_owner].add(slot_share[:, :, None] * expert_y)
    return summed[:length]

def forward(token_f, first_gain, w_query, w_key, w_value, w_out, second_gain, w_router, w_gate, w_up, w_down, routes):
    gain_one = low(first_gain)
    gain_two = low(second_gain)
    query_w = low(w_query)
    key_w = low(w_key)
    value_w = low(w_value)
    out_w = low(w_out)
    router_w = low(w_router)
    gate_w = low(w_gate)
    up_w = low(w_up)
    down_w = low(w_down)
    normed_one = low(token_f * rms_scale(token_f) * gain_one)
    query_rows = low_back(jnp.dot(normed_one, query_w, precision=highest)).reshape(TOKENS, H, HD)
    key_rows = low_back(jnp.dot(normed_one, key_w, precision=highest)).reshape(TOKENS, KV, HD)
    value_rows = low(low_back(jnp.dot(normed_one, value_w, precision=highest))).reshape(TOKENS, KV, HD)
    positions = (jnp.arange(TOKENS, dtype=jnp.int32) % TOK_DEV).astype(jnp.float32)
    cosine, sine_tab = rope_tables(positions)
    query_rows = low(rotate(query_rows, cosine, sine_tab))
    key_rows = low(rotate(key_rows, cosine, sine_tab))
    mixed = lax.map(jax.checkpoint(attend_one), (query_rows.reshape(N_GX, TOK_DEV, H, HD), key_rows.reshape(N_GX, TOK_DEV, KV, HD), value_rows.reshape(N_GX, TOK_DEV, KV, HD)))
    mixed = low(low_back(mixed.reshape(TOKENS, H * HD)))
    attn_out = low_back(jnp.dot(mixed, out_w.T, precision=highest))
    residual = token_f + attn_out
    normed_two = low(residual * rms_scale(residual) * gain_two)
    logits = low_back(jnp.dot(normed_two, router_w, precision=highest))
    gate_probs = jax.nn.softmax(jnp.take_along_axis(logits, routes, axis=1), axis=-1)

    def mix_sequence(batch_items):
        return mix_one(batch_items[0], batch_items[1], batch_items[2], gate_w, up_w, down_w)
    expert_out = lax.map(jax.checkpoint(mix_sequence), (normed_two.reshape(N_GX, TOK_DEV, D), gate_probs.reshape(N_GX, TOK_DEV, TOP), routes.reshape(N_GX, TOK_DEV, TOP)))
    return residual + expert_out.reshape(TOKENS, D)

def reference(tokens, first_gain, w_query, w_key, w_value, w_out, second_gain, w_router, w_gate, w_up, w_down, routes, block_cotangent):

    def apply_layer(token_f, gain_one, query_w, key_w, value_w, out_w, gain_two, router_w, gate_w, up_w, down_w):
        return forward(token_f, gain_one, query_w, key_w, value_w, out_w, gain_two, router_w, gate_w, up_w, down_w, routes)
    token_f = tokens.astype(jnp.float32)
    result, pullback = jax.vjp(apply_layer, token_f, first_gain, w_query, w_key, w_value, w_out, second_gain, w_router, w_gate, w_up, w_down)
    gradients = pullback(block_cotangent.astype(jnp.float32))
    return (result.astype(jnp.bfloat16), gradients[0].astype(jnp.bfloat16), gradients[1], gradients[2], gradients[3], gradients[4], gradients[5], gradients[6], gradients[7], gradients[8], gradients[9], gradients[10])
```

```python
from functools import partial
import math

import jax
import jax.numpy as jnp
import numpy as np
from jax import lax
from jax.experimental import pallas as pl
from jax.experimental.pallas import tpu as pltpu
from jax.sharding import PartitionSpec as P

D = 1536
HD = 64
FFZ = 128
epsilon = 1e-06
rope_base = 10000.0
masked = -1e30
BF = jnp.bfloat16
F32 = jnp.float32


def dot(a, b, dims=((1,), (0,)), out=F32):
    return lax.dot_general(a, b, (dims, ((), ())), preferred_element_type=F32).astype(out)


def flip(bit, size):
    return [(i, i ^ bit) for i in range(size)]


def swap_core(x):
    return lax.ppermute(x, "gx", flip(1, lax.axis_size("gx")))


def swap_x(x):
    return lax.ppermute(x, "gx", flip(2, lax.axis_size("gx")))


def swap_y(x):
    return lax.ppermute(x, "gx", flip(4, lax.axis_size("gx")))


def core_groups(size):
    return [[i for i in range(size) if i % 2 == c] for c in range(2)]


def place_chips(chunks, chip):
    rows = chunks[0].shape[0]
    whole = jnp.zeros((4 * rows, chunks[0].shape[1]), chunks[0].dtype)
    for k, part in enumerate(chunks):
        whole = lax.dynamic_update_slice(whole, part, ((chip ^ k) * rows, 0))
    return whole


def gather_chips(own):
    size = lax.axis_size("gx")
    if size != 8:
        return lax.all_gather(own, "gx", axis=0, tiled=True, axis_index_groups=core_groups(size))
    half = own.shape[1] // 2
    from_x = swap_x(own)
    from_y = swap_y(own)
    corner = jnp.concatenate([swap_y(from_x[:, :half]), swap_x(from_y[:, half:])], axis=1)
    return place_chips([own, from_x, from_y, corner], lax.axis_index("gx") // 2)


def reduce_chips(term, rows, half):
    size = lax.axis_size("gx")
    chip = lax.axis_index("gx") // 2
    if size != 8:
        whole = jnp.concatenate([term(0, rows * size // 2, 0), term(0, rows * size // 2, 1)], axis=1)
        return lax.psum_scatter(
            whole, "gx", scatter_dimension=0, tiled=True, axis_index_groups=core_groups(size)
        )
    a1, a3 = term((chip ^ 1) * rows, rows, 0), term((chip ^ 3) * rows, rows, 0)
    b2, b3 = term((chip ^ 2) * rows, rows, 1), term((chip ^ 3) * rows, rows, 1)
    got_a0, got_a2 = swap_x(a1), swap_x(a3)
    got_b0, got_b1 = swap_y(b2), swap_y(b3)
    a0, a2 = term(chip * rows, rows, 0), term((chip ^ 2) * rows, rows, 0)
    b0, b1 = term(chip * rows, rows, 1), term((chip ^ 1) * rows, rows, 1)
    last_a, last_b = swap_y(a2 + got_a2), swap_x(b1 + got_b1)
    side_a = a0.astype(F32) + got_a0 + last_a
    side_b = b0.astype(F32) + got_b0 + last_b
    return jnp.concatenate([side_a, side_b], axis=1).astype(BF)


def rope_tables(length):
    frequency = np.exp(np.arange(HD // 2, dtype=np.float32) * np.float32(-2.0 * math.log(rope_base) / HD))
    angles = np.arange(length, dtype=np.float32)[:, None] * frequency[None, :].astype(np.float32)
    return (jnp.asarray(np.cos(angles), F32)[:, None, :], jnp.asarray(np.sin(angles), F32)[:, None, :])


def rotate(values, cosine, sine_tab):
    half_width = values.shape[-1] // 2
    first_half = values[..., :half_width]
    second_half = values[..., half_width:]
    return jnp.concatenate(
        [
            first_half * cosine - second_half * sine_tab,
            second_half * cosine + first_half * sine_tab,
        ],
        axis=-1,
    )


def block_scores(query_block, key_rows, first_row, score_scale):
    scores = (
        jnp.einsum("qkgd,tkd->kgqt", query_block, key_rows, preferred_element_type=jnp.float32)
        * score_scale
    )
    row_ids = first_row + lax.broadcasted_iota(jnp.int32, scores.shape, 2)
    col_ids = lax.broadcasted_iota(jnp.int32, scores.shape, 3)
    return jnp.where(col_ids <= row_ids, scores, masked)


def attend(query_rows, key_rows, value_rows, score_scale, block_rows):
    length = query_rows.shape[0]

    def one_block(number):
        first_row = number * block_rows
        query_block = lax.dynamic_slice_in_dim(query_rows, first_row, block_rows, 0)
        scores = block_scores(query_block, key_rows, first_row, score_scale)
        top_score = jnp.max(scores, axis=3, keepdims=True)
        expo_score = jnp.exp(scores - top_score)
        row_sum = jnp.sum(expo_score, axis=3, keepdims=True)
        attn_probs = (expo_score / row_sum).astype(jnp.bfloat16)
        mixed = jnp.einsum(
            "kgqt,tkd->qkgd", attn_probs, value_rows, preferred_element_type=jnp.float32
        )
        return (mixed, (top_score + jnp.log(row_sum))[..., 0])

    mixed, log_total = lax.map(one_block, jnp.arange(length // block_rows))
    return (mixed.reshape(length, -1), log_total)


def attend_back(query_rows, key_rows, value_rows, grad_mixed, log_total, score_scale, block_rows):
    length = query_rows.shape[0]

    def one_block(carried, number):
        grad_keys, grad_values = carried
        first_row = number * block_rows
        query_block = lax.dynamic_slice_in_dim(query_rows, first_row, block_rows, 0)
        grad_block = lax.dynamic_slice_in_dim(grad_mixed, first_row, block_rows, 0)
        scores = block_scores(query_block, key_rows, first_row, score_scale)
        attn_probs = jnp.exp(scores - log_total[number][..., None])
        grad_probs = jnp.einsum(
            "qkgd,tkd->kgqt", grad_block, value_rows, preferred_element_type=jnp.float32
        )
        inner_sum = jnp.sum(attn_probs * grad_probs, axis=3, keepdims=True)
        grad_scores = (attn_probs * (grad_probs - inner_sum)).astype(jnp.bfloat16)
        grad_query = (
            jnp.einsum("kgqt,tkd->qkgd", grad_scores, key_rows, preferred_element_type=jnp.float32)
            * score_scale
        )
        grad_keys = (
            grad_keys
            + jnp.einsum(
                "kgqt,qkgd->tkd", grad_scores, query_block, preferred_element_type=jnp.float32
            )
            * score_scale
        )
        grad_values = grad_values + jnp.einsum(
            "kgqt,qkgd->tkd",
            attn_probs.astype(jnp.bfloat16),
            grad_block,
            preferred_element_type=jnp.float32,
        )
        return ((grad_keys, grad_values), grad_query)

    initial = (jnp.zeros(key_rows.shape, jnp.float32), jnp.zeros(value_rows.shape, jnp.float32))
    (grad_keys, grad_values), grad_query = lax.scan(
        one_block, initial, jnp.arange(length // block_rows)
    )
    return (grad_query.reshape(query_rows.shape), grad_keys, grad_values)


def expert_body(h_ref, wg_ref, wu_ref, draw_ref, gate_ref, dg_ref, du_ref, ga_ref, dsum_ref):
    step = pl.program_id(1)
    h = h_ref[...]
    g = jnp.dot(h, wg_ref[...], preferred_element_type=F32)
    u = jnp.dot(h, wu_ref[...], preferred_element_type=F32)
    lanes = lax.broadcasted_iota(jnp.int32, gate_ref.shape, 1)
    sums = dsum_ref[...]
    sums = jnp.where(step == 0, jnp.zeros_like(sums), sums)
    for half in range(2):
        cols = slice(half * FFZ, (half + 1) * FFZ)
        expert = step * 2 + half
        hot = lanes == expert
        gate = jnp.sum(jnp.where(hot, gate_ref[...], 0.0), axis=1, keepdims=True)
        gg, uu = g[:, cols], u[:, cols]
        draw = draw_ref[:, cols].astype(F32)
        sig = 1.0 / (1.0 + jnp.exp(-gg))
        silu = gg * sig
        act = silu * uu
        back = gate * draw
        ga_ref[:, cols] = (gate * act).astype(BF)
        du_ref[:, cols] = (back * silu).astype(BF)
        dg_ref[:, cols] = (back * uu * (sig + silu * (1.0 - sig))).astype(BF)
        sums = jnp.where(hot, jnp.sum(act * draw, axis=1, keepdims=True), sums)
    dsum_ref[...] = sums


def expert_forward(h, w_gate, w_up, draw, gate):
    tokens, width = draw.shape
    rows = 1024
    steps = width // (2 * FFZ)
    wide = pl.BlockSpec((rows, 2 * FFZ), lambda i, j: (i, j))
    weight = pl.BlockSpec((D, 2 * FFZ), lambda i, j: (0, j))
    small = pl.BlockSpec((rows, 128), lambda i, j: (i, 0))
    return pl.pallas_call(
        expert_body,
        grid=(tokens // rows, steps),
        in_specs=[pl.BlockSpec((rows, D), lambda i, j: (i, 0)), weight, weight, wide, small],
        out_specs=[wide, wide, wide, small],
        out_shape=[jax.ShapeDtypeStruct((tokens, width), BF)] * 3
        + [jax.ShapeDtypeStruct((tokens, 128), F32)],
        compiler_params=pltpu.CompilerParams(vmem_limit_bytes=56 * 1024 * 1024),
        cost_estimate=pl.CostEstimate(
            flops=4 * tokens * D * width, bytes_accessed=tokens * width * 8 + D * width * 8, transcendentals=tokens * width
        ),
    )(h, w_gate, w_up, draw, gate)


def pad_lanes(x, width=128):
    return jnp.pad(x, ((0, 0), (0, width - x.shape[1])))


def shards(
    tokens,
    first_gain,
    w_query,
    w_key,
    w_value,
    w_out,
    second_gain,
    w_router,
    w_gate,
    w_up,
    w_down,
    routes,
    block_cotangent,
):
    length = tokens.shape[0]
    rows_here = w_query.shape[0]
    chip_rows = 2 * rows_here
    heads_here = w_query.shape[1] // HD
    groups_here = w_key.shape[1] // HD
    share_heads = heads_here // groups_here
    experts_n = w_router.shape[1]
    mine_n = experts_n // 2
    hidden_here = w_gate.shape[2]
    span = mine_n * hidden_here
    slice_cols = tokens.shape[1]
    block_rows = min(512, length)
    score_scale = HD ** (-0.5)
    core = lax.axis_index("gx") % 2
    plane = lax.axis_index("gy")

    gains = jnp.stack([first_gain, second_gain]).astype(BF)
    gains = jnp.pad(gains, ((0, 14), (0, 0)))
    joined = lax.all_gather(jnp.concatenate([tokens, gains], axis=0), "gy", axis=1, tiled=True)
    token_full = joined[:length]
    gain_full = joined[length : length + 2].astype(F32)
    gain_one, gain_two = gain_full[0], gain_full[1]

    attn_own = jnp.concatenate(
        [w_query.astype(BF), w_key.astype(BF), w_value.astype(BF), w_out.astype(BF), pad_lanes(w_router.astype(BF))],
        axis=1,
    )
    attn_pair = swap_core(attn_own)

    def core_order(own, other):
        first = jnp.where(core == 0, own, other)
        second = jnp.where(core == 0, other, own)
        return first, second

    attn_whole = gather_chips(jnp.concatenate(core_order(attn_own, attn_pair), axis=0))
    query_cols, pair_cols = w_query.shape[1], w_key.shape[1]
    qkv_cols = query_cols + 2 * pair_cols
    qkv_w = attn_whole[:, :qkv_cols]
    out_w = attn_whole[:, qkv_cols : qkv_cols + w_out.shape[1]]
    router_w = attn_whole[:, qkv_cols + w_out.shape[1] :]

    def expert_rows(weight):
        both = weight.astype(BF).reshape(rows_here, 2, span)
        keep = jnp.where(core == 0, both[:, 0], both[:, 1])
        give = jnp.where(core == 0, both[:, 1], both[:, 0])
        return gather_chips(jnp.concatenate(core_order(keep, swap_core(give)), axis=0))

    down_w = expert_rows(w_down)
    gate_w = expert_rows(w_gate)
    up_w = expert_rows(w_up)

    cot_own = lax.all_gather(block_cotangent, "gy", axis=1, tiled=True)
    cot_both = jnp.concatenate([cot_own, swap_core(cot_own)], axis=0)
    down_raw = dot(cot_both, down_w, out=BF)

    iota = jnp.arange(128, dtype=jnp.int32)
    routes_both = jnp.concatenate([routes, swap_core(routes)], axis=0)
    member = jnp.any(routes_both[:, :, None] == iota[None, None, :], axis=1)

    xf = token_full.astype(F32)
    scale_one = lax.rsqrt(jnp.mean(xf * xf, axis=1, keepdims=True) + epsilon)
    normed_one = (xf * scale_one * gain_one).astype(BF)
    qkv_raw = dot(normed_one, qkv_w)
    cosine, sine_tab = rope_tables(length)
    query_rows = rotate(qkv_raw[:, :query_cols].reshape(length, heads_here, HD), cosine, sine_tab).astype(BF)
    key_rows = rotate(
        qkv_raw[:, query_cols : query_cols + pair_cols].reshape(length, groups_here, HD), cosine, sine_tab
    ).astype(BF)
    value_rows = qkv_raw[:, query_cols + pair_cols :].reshape(length, groups_here, HD).astype(BF)
    query_group = query_rows.reshape(length, groups_here, share_heads, HD)
    mixed, log_total = attend(query_group, key_rows, value_rows, score_scale, block_rows)
    mixed = mixed.astype(BF)
    attn_partial = dot(mixed, out_w, ((1,), (1,)), BF)
    attn_slice = lax.psum_scatter(attn_partial, "gy", scatter_dimension=1, tiled=True)
    token_slice = tokens.astype(F32)
    residual = token_slice + attn_slice.astype(F32)
    residual_own = lax.all_gather(residual.astype(BF), "gy", axis=1, tiled=True)
    residual_both = jnp.concatenate([residual_own, swap_core(residual_own)], axis=0)

    rf = residual_both.astype(F32)
    scale_two = lax.rsqrt(jnp.mean(rf * rf, axis=1, keepdims=True) + epsilon)
    normed_two = (rf * scale_two * gain_two).astype(BF)
    logits = jnp.where(member, dot(normed_two, router_w), masked)
    gate_exp = jnp.exp(logits - jnp.max(logits, axis=1, keepdims=True))
    gate_all = gate_exp / jnp.sum(gate_exp, axis=1, keepdims=True)
    gate_mine = pad_lanes(lax.dynamic_slice_in_dim(gate_all, core * mine_n, mine_n, 1))
    grad_gate, grad_up, gated, dsum = expert_forward(normed_two, gate_w, up_w, down_raw, gate_mine)

    dsum_own, dsum_got = dsum[:length, :mine_n], swap_core(dsum[length:, :mine_n])
    dsum_pair = jnp.concatenate(core_order(dsum_own, dsum_got), axis=1).T
    dsum_all = jnp.sum(lax.all_gather(dsum_pair, "gy", axis=0), axis=0).T
    gate_own = gate_all[:length, :experts_n]
    grad_picked = gate_own * (dsum_all - jnp.sum(gate_own * dsum_all, axis=1, keepdims=True))
    grad_logits = grad_picked.astype(BF)

    def back_half(rows):
        return (
            dot(grad_gate[rows], gate_w, ((1,), (1,))) + dot(grad_up[rows], up_w, ((1,), (1,)))
        ).astype(BF)

    back_other = swap_core(back_half(slice(length, 2 * length)))
    back_own = back_half(slice(0, length))
    back_sum = (back_own.astype(F32) + back_other.astype(F32)).astype(BF)
    router_slice = lax.dynamic_slice_in_dim(router_w[:, :experts_n], plane * slice_cols, slice_cols, 0)
    grad_normed_two = lax.psum_scatter(back_sum, "gy", scatter_dimension=1, tiled=True).astype(F32) + dot(
        grad_logits, router_slice, ((1,), (1,))
    )
    grad_h2_full = lax.all_gather(grad_normed_two.astype(BF), "gy", axis=1, tiled=True)

    def column_term(left, right):
        half = right.shape[1] // 2

        def term(first_row, rows, side):
            return dot(
                lax.dynamic_slice_in_dim(left, first_row, rows, 1),
                right[:, side * half : (side + 1) * half],
                ((0,), (0,)),
                BF,
            )

        return term

    def expert_grad(left, right):
        total = reduce_chips(column_term(left, right), chip_rows, span // 2)
        keep = jnp.where(core == 0, total[:rows_here], total[rows_here:])
        give = jnp.where(core == 0, total[rows_here:], total[:rows_here])
        both = jnp.concatenate(core_order(keep, swap_core(give)), axis=1)
        return both.reshape(rows_here, experts_n, hidden_here).astype(F32)

    down_grad = expert_grad(cot_both, gated)
    gate_grad = expert_grad(normed_two, grad_gate)
    up_grad = expert_grad(normed_two, grad_up)
    router_grad = lax.psum_scatter(
        dot(normed_two[:length], grad_logits, ((0,), (0,)), BF), "gx", scatter_dimension=0, tiled=True
    ).astype(F32)

    moe_other = swap_core(dot(gated[length:], down_w, ((1,), (1,)), BF))
    moe_own = (dot(gated[:length], down_w, ((1,), (1,))) + moe_other.astype(F32)).astype(BF)
    moe_slice = lax.psum_scatter(moe_own, "gy", scatter_dimension=1, tiled=True)
    block_out = (residual + moe_slice.astype(F32)).astype(BF)

    scale_own = scale_two[:length]
    grad_h2_f = grad_h2_full.astype(F32)
    inner = jnp.sum(grad_h2_f * gain_two * rf[:length], axis=1, keepdims=True)
    grad_res_full = (
        cot_own.astype(F32)
        + scale_own * grad_h2_f * gain_two
        - rf[:length] * scale_own * scale_own * scale_own * inner / D
    ).astype(BF)
    gain_two_slice = second_gain.astype(BF).astype(F32)
    grad_residual = (
        block_cotangent.astype(F32)
        + scale_own * grad_normed_two * gain_two_slice
        - residual * scale_own * scale_own * scale_own * inner / D
    )
    second_gain_grad = jnp.sum(grad_normed_two * residual * scale_own, axis=0)

    grad_mixed = dot(grad_res_full, out_w, out=BF)
    grad_query, grad_keys, grad_values = attend_back(
        query_group,
        key_rows,
        value_rows,
        grad_mixed.reshape(length, groups_here, share_heads, HD),
        log_total,
        score_scale,
        block_rows,
    )
    grad_q_raw = (
        rotate(grad_query.reshape(length, heads_here, HD), cosine, -sine_tab).astype(BF).reshape(length, -1)
    )
    grad_k_raw = rotate(grad_keys, cosine, -sine_tab).astype(BF).reshape(length, -1)
    grad_v_raw = grad_values.astype(BF).reshape(length, -1)
    grad_qkv = jnp.concatenate([grad_q_raw, grad_k_raw, grad_v_raw], axis=1)

    grad_normed_one = lax.psum_scatter(
        dot(grad_qkv, qkv_w, ((1,), (1,)), BF), "gy", scatter_dimension=1, tiled=True
    ).astype(F32)

    out_sum = lax.psum_scatter(
        dot(grad_res_full, mixed, ((0,), (0,)), BF), "gx", scatter_dimension=0, tiled=True
    ).astype(F32)
    qkv_sum = lax.psum_scatter(
        dot(normed_one, grad_qkv, ((0,), (0,)), BF), "gx", scatter_dimension=0, tiled=True
    ).astype(F32)
    query_grad = qkv_sum[:, :query_cols]
    key_grad = qkv_sum[:, query_cols : query_cols + pair_cols]
    value_grad = qkv_sum[:, query_cols + pair_cols :]

    gain_one_slice = first_gain.astype(BF).astype(F32)
    scaled = grad_normed_one * gain_one_slice
    inner_one = lax.psum(jnp.sum(scaled * token_slice, axis=1), "gy")[:, None]
    input_grad = (
        grad_residual
        + scale_one * scaled
        - token_slice * scale_one * scale_one * scale_one * inner_one / D
    ).astype(BF)
    first_gain_grad = jnp.sum(grad_normed_one * token_slice * scale_one, axis=0)
    first_gain_grad, second_gain_grad = lax.psum((first_gain_grad, second_gain_grad), "gx")
    return (
        block_out,
        input_grad,
        first_gain_grad,
        query_grad,
        key_grad,
        value_grad,
        out_sum,
        second_gain_grad,
        router_grad,
        gate_grad,
        up_grad,
        down_grad,
    )


def solution(mesh):
    placed = (
        P("gx", "gy"),
        P("gy"),
        P("gx", "gy"),
        P("gx", "gy"),
        P("gx", "gy"),
        P("gx", "gy"),
        P("gy"),
        P("gx", None),
        P("gx", None, "gy"),
        P("gx", None, "gy"),
        P("gx", None, "gy"),
        P("gx", None),
        P("gx", "gy"),
    )
    return jax.shard_map(
        shards,
        mesh=mesh,
        in_specs=placed,
        out_specs=(
            P("gx", "gy"),
            P("gx", "gy"),
            P("gy"),
            P("gx", "gy"),
            P("gx", "gy"),
            P("gx", "gy"),
            P("gx", "gy"),
            P("gy"),
            P("gx", None),
            P("gx", None, "gy"),
            P("gx", None, "gy"),
            P("gx", None, "gy"),
        ),
        check_vma=False,
    )
```

```python
from functools import partial
import math

import jax
import jax.numpy as jnp
import numpy as np
from jax import lax
from jax.experimental import pallas as pl
from jax.experimental.pallas import tpu as pltpu
from jax.sharding import PartitionSpec as P

D = 1536
HD = 64
FFZ = 128
epsilon = 1e-06
BF = jnp.bfloat16
F32 = jnp.float32
masked = -1e30
VM = pl.BlockSpec(memory_space=pltpu.VMEM)
MB = 1024 * 1024

def rope_tables(length):
    frequency = np.exp(np.arange(HD // 2) * (-2.0 * math.log(10000.0) / HD)).astype(np.float32)
    angles = np.arange(length, dtype=np.float32)[:, None] * frequency[None, :]
    cosine, sine_tab = np.cos(angles), np.sin(angles)
    return (
        jnp.asarray(np.concatenate([cosine, cosine], axis=1), F32),
        jnp.asarray(np.concatenate([-sine_tab, sine_tab], axis=1), F32),
    )

def halves_swapped(x):
    return jnp.concatenate([x[:, HD // 2 :], x[:, : HD // 2]], axis=1)

def causal_scores(q, keys, first):
    rows, length = q.shape[0], keys.shape[0]
    scores = lax.dot_general(q, keys, (((1,), (1,)), ((), ())), preferred_element_type=F32)
    row_ids = first + lax.broadcasted_iota(jnp.int32, (rows, length), 0)
    col_ids = lax.broadcasted_iota(jnp.int32, (rows, length), 1)
    return jnp.where(col_ids <= row_ids, scores, masked)

def attend_body(heads, groups, block, qkv_ref, cos_ref, sin_ref, mixed_ref, q_ref, k_ref, v_ref, log_ref, mixed_scr):
    length = qkv_ref.shape[0]
    cosine, sine = cos_ref[...], sin_ref[...]
    for h in range(heads + groups):
        x = qkv_ref[:, h * HD : (h + 1) * HD]
        x = (x * cosine + halves_swapped(x) * sine).astype(BF)
        if h < heads:
            q_ref[h] = x * jnp.asarray(HD**-0.5, BF)
        else:
            k_ref[h - heads] = x
    for g in range(groups):
        at = (heads + groups + g) * HD
        v_ref[g] = qkv_ref[:, at : at + HD].astype(BF)
    log_ref[...] = jnp.zeros_like(log_ref)
    share = heads // groups

    def head(h, carry):
        group = h // share
        for i in range(length // block):
            rows = slice(i * block, (i + 1) * block)
            seen = slice(0, (i + 1) * block)
            scores = causal_scores(q_ref[h, rows], k_ref[group, seen], i * block)
            top = jnp.max(scores, axis=1, keepdims=True)
            expo = jnp.exp(scores - top)
            total = jnp.sum(expo, axis=1, keepdims=True)
            probs = (expo * (1.0 / total)).astype(BF)
            mixed_scr[h, rows] = jnp.dot(probs, v_ref[group, seen], preferred_element_type=F32).astype(BF)
            lanes = lax.broadcasted_iota(jnp.int32, (block, 128), 1)
            log_ref[rows] = jnp.where(lanes == h, top + jnp.log(total), log_ref[rows])
        return carry

    lax.fori_loop(0, heads, head, 0)
    for h in range(0, heads, 2):
        mixed_ref[:, h * HD : (h + 2) * HD] = jnp.concatenate([mixed_scr[h], mixed_scr[h + 1]], axis=1)

def attend(qkv, heads, groups, block=256):
    length = qkv.shape[0]
    cosine, sine = rope_tables(length)
    S = jax.ShapeDtypeStruct
    return pl.pallas_call(
        partial(attend_body, heads, groups, block),
        in_specs=[VM] * 3,
        out_specs=[VM] * 5,
        out_shape=[
            S((length, heads * HD), BF),
            S((heads, length, HD), BF),
            S((groups, length, HD), BF),
            S((groups, length, HD), BF),
            S((length, 128), F32),
        ],
        scratch_shapes=[pltpu.VMEM((heads, length, HD), BF)],
        compiler_params=pltpu.CompilerParams(vmem_limit_bytes=40 * MB),
    )(qkv, cosine, sine)

def attend_back_body(heads, groups, block, q_ref, k_ref, v_ref, log_ref, mixed_ref, do_ref, cos_ref, sin_ref, out_ref, do_scr, mixed_scr, dq_scr, dk_scr, dv_scr):
    length = do_ref.shape[0]
    share = heads // groups
    for h in range(heads):
        do_scr[h] = do_ref[:, h * HD : (h + 1) * HD]
        mixed_scr[h] = mixed_ref[:, h * HD : (h + 1) * HD]
    dk_scr[...] = jnp.zeros_like(dk_scr)
    dv_scr[...] = jnp.zeros_like(dv_scr)

    def head(h, carry):
        group = h // share
        for i in range(length // block):
            rows = slice(i * block, (i + 1) * block)
            seen = slice(0, (i + 1) * block)
            q, keys, values, do = q_ref[h, rows], k_ref[group, seen], v_ref[group, seen], do_scr[h, rows]
            lanes = lax.broadcasted_iota(jnp.int32, (block, 128), 1)
            log_total = jnp.sum(jnp.where(lanes == h, log_ref[rows], 0.0), axis=1, keepdims=True)
            probs = jnp.exp(causal_scores(q, keys, i * block) - log_total)
            grad_probs = lax.dot_general(do, values, (((1,), (1,)), ((), ())), preferred_element_type=F32)
            inner = jnp.sum(do.astype(F32) * mixed_scr[h, rows].astype(F32), axis=1, keepdims=True)
            grad_scores = (probs * (grad_probs - inner)).astype(BF)
            dq_scr[h, rows] = jnp.dot(grad_scores, keys, preferred_element_type=F32) * (HD**-0.5)
            across = (((0,), (0,)), ((), ()))
            dk_scr[group, seen] += lax.dot_general(grad_scores, q, across, preferred_element_type=F32)
            dv_scr[group, seen] += lax.dot_general(probs.astype(BF), do, across, preferred_element_type=F32)
        return carry

    lax.fori_loop(0, heads, head, 0)
    cosine, sine = cos_ref[...], sin_ref[...]

    def back(x):
        return (x * cosine - halves_swapped(x) * sine).astype(BF)

    cols = [back(dq_scr[h]) for h in range(heads)]
    cols += [back(dk_scr[g]) for g in range(groups)]
    cols += [dv_scr[g].astype(BF) for g in range(groups)]
    for p in range(0, len(cols), 2):
        out_ref[:, p * HD : (p + 2) * HD] = jnp.concatenate([cols[p], cols[p + 1]], axis=1)

def attend_back(q, k, v, log_total, mixed, do, block=256):
    heads, length, _ = q.shape
    groups = k.shape[0]
    cosine, sine = rope_tables(length)
    return pl.pallas_call(
        partial(attend_back_body, heads, groups, block),
        in_specs=[VM] * 8,
        out_specs=VM,
        out_shape=jax.ShapeDtypeStruct((length, (heads + 2 * groups) * HD), BF),
        scratch_shapes=[
            pltpu.VMEM((heads, length, HD), BF),
            pltpu.VMEM((heads, length, HD), BF),
            pltpu.VMEM((heads, length, HD), F32),
            pltpu.VMEM((groups, length, HD), F32),
            pltpu.VMEM((groups, length, HD), F32),
        ],
        compiler_params=pltpu.CompilerParams(vmem_limit_bytes=48 * MB),
    )(q, k, v, log_total, mixed, do, cosine, sine)

def expert_math(gate, draw, gg, uu):
    sig = 1.0 / (1.0 + jnp.exp(-gg))
    silu = gg * sig
    act = silu * uu
    back = gate * draw
    return (
        (gate * act).astype(BF),
        (back * uu * (sig + silu * (1.0 - sig))).astype(BF),
        (back * silu).astype(BF),
        jnp.sum(act * draw, axis=1, keepdims=True),
    )

def expert_body(rows, chunk, h_ref, wg_ref, wu_ref, draw_ref, gate_ref, out_ref, dsum_ref):
    step = pl.program_id(1)
    wg, wu = wg_ref[...], wu_ref[...]
    for m in range(rows // chunk):
        at = slice(m * chunk, (m + 1) * chunk)
        h = h_ref[at]
        g = jnp.dot(h, wg, preferred_element_type=F32)
        u = jnp.dot(h, wu, preferred_element_type=F32)
        lanes = lax.broadcasted_iota(jnp.int32, (chunk, 128), 1)
        gates = gate_ref[at]
        sums = jnp.where(step == 0, 0.0, dsum_ref[at])
        for half in range(2):
            cols = slice(half * FFZ, (half + 1) * FFZ)
            hot = lanes == step * 2 + half
            gate = jnp.sum(jnp.where(hot, gates, 0.0), axis=1, keepdims=True)
            ga, dg, du, s = expert_math(gate, draw_ref[at, cols].astype(F32), g[:, cols], u[:, cols])
            out_ref[0, at, cols] = ga
            out_ref[1, at, cols] = dg
            out_ref[2, at, cols] = du
            sums = jnp.where(hot, s, sums)
        dsum_ref[at] = sums

def expert_forward(h, w_all, draw, gate, rows=1024, chunk=256):
    tokens, width = draw.shape
    steps = width // (2 * FFZ)
    return pl.pallas_call(
        partial(expert_body, rows, chunk),
        grid=(tokens // rows, steps),
        in_specs=[
            pl.BlockSpec((rows, D), lambda i, j: (i, 0)),
            pl.BlockSpec((D, 2 * FFZ), lambda i, j: (0, steps + j)),
            pl.BlockSpec((D, 2 * FFZ), lambda i, j: (0, 2 * steps + j)),
            pl.BlockSpec((rows, 2 * FFZ), lambda i, j: (i, j)),
            pl.BlockSpec((rows, 128), lambda i, j: (i, 0)),
        ],
        out_specs=[
            pl.BlockSpec((3, rows, 2 * FFZ), lambda i, j: (0, i, j)),
            pl.BlockSpec((rows, 128), lambda i, j: (i, 0)),
        ],
        out_shape=[
            jax.ShapeDtypeStruct((3, tokens, width), BF),
            jax.ShapeDtypeStruct((tokens, 128), F32),
        ],
        compiler_params=pltpu.CompilerParams(vmem_limit_bytes=56 * MB),
    )(h, w_all, w_all, draw, gate)

def project_body(n, *refs):
    dims = (((1,), (1,)), ((), ()))
    o_ref = refs[2 * n]
    total = None
    for a_ref, w_ref in zip(refs[:n], refs[n : 2 * n]):
        a = a_ref[0] if len(a_ref.shape) == 3 else a_ref[...]
        term = lax.dot_general(a, w_ref[...], dims, preferred_element_type=F32)
        total = term if total is None else total + term
    cols = o_ref.shape[2]
    o_ref[0] = total[:, :cols].astype(BF)
    o_ref[1] = total[:, cols:].astype(BF)

def project(terms, parts):
    rows, width = terms[0][1][-2:]
    cols = D // parts
    n = len(terms)
    total = pl.pallas_call(
        partial(project_body, n),
        grid=(parts // 2,),
        in_specs=[pl.BlockSpec(t[1], partial(lambda at, j: at, t[2])) for t in terms]
        + [pl.BlockSpec((2 * cols, width), partial(lambda at, j: (j, at), t[4])) for t in terms],
        out_specs=pl.BlockSpec((2, rows, cols), lambda j: (j, 0, 0)),
        out_shape=jax.ShapeDtypeStruct((parts, rows, cols), BF),
        compiler_params=pltpu.CompilerParams(vmem_limit_bytes=56 * MB),
    )(*[t[0] for t in terms], *[t[3] for t in terms])
    return total.reshape(parts * rows, cols)

def term_body(steps, ids_ref, c0_ref, c1_ref, h0_ref, h1_ref, g_ref, a_ref, b_ref):
    side, m = pl.program_id(0), pl.program_id(1)
    rows = c0_ref.shape[1]
    across = (((0,), (0,)), ((), ()))

    def work(l0, l1, o_ref):
        g = g_ref[0]
        o_ref[:rows] = lax.dot_general(l0[...], g, across, preferred_element_type=F32).astype(BF)
        o_ref[rows:] = lax.dot_general(l1[...], g, across, preferred_element_type=F32).astype(BF)

    for s, o_ref in ((0, a_ref), (1, b_ref)):
        @pl.when((side == s) & (m == 0))
        def _():
            work(c0_ref, c1_ref, o_ref)

        @pl.when((side == s) & (m > 0))
        def _():
            work(h0_ref, h1_ref, o_ref)

def expert_terms(ids, c, h, grads, rows, cols=1280):
    tokens, width = grads.shape[1:]
    steps = width // 2 // cols
    last = 3 * steps - 1
    piece = lambda p: pl.BlockSpec((tokens, rows), lambda s, m, j, ids: (0, ids[2 * s + p]))
    out = jax.ShapeDtypeStruct((2 * rows, 3 * width // 2), BF)
    return pl.pallas_call(
        partial(term_body, steps),
        grid_spec=pltpu.PrefetchScalarGridSpec(
            num_scalar_prefetch=1,
            grid=(2, 3, steps),
            in_specs=[piece(0), piece(1), piece(0), piece(1),
                pl.BlockSpec((1, tokens, cols), lambda s, m, j, ids: (m, 0, s * steps + j))],
            out_specs=[
                pl.BlockSpec((2 * rows, cols), lambda s, m, j, ids: (0, jnp.where(s == 0, m * steps + j, last))),
                pl.BlockSpec((2 * rows, cols), lambda s, m, j, ids: (0, jnp.where(s == 0, 0, m * steps + j))),
            ],
        ),
        out_shape=[out, out],
        compiler_params=pltpu.CompilerParams(vmem_limit_bytes=56 * MB),
    )(ids, c, c, h, h, grads)

def prepare_body(core_ref, down_ref, gate_ref, up_ref, keep_ref, give_ref):
    first = core_ref[0] == 0
    rows, n2, _ = down_ref.shape
    n = n2 // 2
    for m, ref in enumerate((down_ref, gate_ref, up_ref)):
        flat = ref.reshape(rows * n2, FFZ)
        for e in range(n):
            lo = flat[pl.ds(e, rows, stride=n2), :]
            hi = flat[pl.ds(n + e, rows, stride=n2), :]
            at = (m * n + e) * FFZ
            keep_ref[:, at : at + FFZ] = jnp.where(first, lo, hi).astype(BF)
            give_ref[:, at : at + FFZ] = jnp.where(first, hi, lo).astype(BF)

def prepare(core, down, gate, up):
    rows, n, _ = down.shape
    part = 48
    wide = 3 * n * FFZ // 2
    weight = pl.BlockSpec((part, n, FFZ), lambda i, c: (i, 0, 0))
    out = pl.BlockSpec((part, wide), lambda i, c: (i, 0))
    return pl.pallas_call(
        prepare_body,
        grid_spec=pltpu.PrefetchScalarGridSpec(num_scalar_prefetch=1, grid=(rows // part,), in_specs=[weight] * 3, out_specs=[out] * 2),
        out_shape=[jax.ShapeDtypeStruct((rows, wide), BF)] * 2,
        compiler_params=pltpu.CompilerParams(vmem_limit_bytes=40 * MB),
    )(core, down, gate, up)

def place_body(offs_ref, *refs):
    fulls, lefts, rights, out = refs[:6], refs[6:8], refs[8:10], refs[10]
    rows = fulls[0].shape[0]

    def put(i, ref):
        out[pl.ds(pl.multiple_of(offs_ref[i] * rows, 16), rows), :] = ref[...]

    for i, ref in enumerate(fulls):
        put(i, ref)
    left = pl.program_id(0) < pl.num_programs(0) // 2

    @pl.when(left)
    def _():
        for i, ref in enumerate(lefts):
            put(6 + i, ref)

    @pl.when(jnp.logical_not(left))
    def _():
        for i, ref in enumerate(rights):
            put(6 + i, ref)

def place(offsets, fulls, lefts, rights, steps=10):
    rows, wide = fulls[0].shape
    cols = wide // steps
    half = steps // 2
    return pl.pallas_call(
        place_body,
        grid_spec=pltpu.PrefetchScalarGridSpec(
            num_scalar_prefetch=1,
            grid=(steps,),
            in_specs=[pl.BlockSpec((rows, cols), lambda j, o: (0, j))] * 6
            + [pl.BlockSpec((rows, cols), lambda j, o: (0, jnp.minimum(j, half - 1)))] * 2
            + [pl.BlockSpec((rows, cols), lambda j, o: (0, jnp.maximum(j - half, 0)))] * 2,
            out_specs=pl.BlockSpec((8 * rows, cols), lambda j, o: (0, j)),
        ),
        out_shape=jax.ShapeDtypeStruct((8 * rows, wide), fulls[0].dtype),
        compiler_params=pltpu.CompilerParams(vmem_limit_bytes=40 * MB),
    )(offsets, *fulls, *lefts, *rights)

def finish_body(core_ref, *refs):
    n_own = (len(refs) - 5) // 2
    own_a, own_b = refs[:n_own], refs[n_own : 2 * n_own]
    got_a, got_b = refs[2 * n_own], refs[2 * n_own + 1]
    outs = refs[2 * n_own + 2 :]
    first = core_ref[0] == 0
    rows, n4, _ = outs[0].shape
    n = n4 // 4
    for m, out in enumerate(outs):
        flat = out.reshape(rows * n4, FFZ)
        for s, (own, got) in enumerate(((own_a, got_a), (own_b, got_b))):
            for e in range(n):
                cols = slice((m * n + e) * FFZ, (m * n + e + 1) * FFZ)
                mine = own[0][:, cols].astype(F32)
                for ref in own[1:]:
                    mine = mine + ref[:, cols].astype(F32)
                theirs = got[:, cols].astype(F32)
                flat[pl.ds(s * n + e, rows, stride=n4), :] = jnp.where(first, mine, theirs)
                flat[pl.ds(2 * n + s * n + e, rows, stride=n4), :] = jnp.where(first, theirs, mine)

def finish(core, own_a, own_b, got_a, got_b, experts):
    rows, wide = got_a.shape
    part = 48
    steps = rows // part
    own = pl.BlockSpec((part, wide), lambda i, c: (c[0] * steps + i, 0))
    got = pl.BlockSpec((part, wide), lambda i, c: (i, 0))
    out = pl.BlockSpec((part, experts, FFZ), lambda i, c: (i, 0, 0))
    return pl.pallas_call(
        finish_body,
        grid_spec=pltpu.PrefetchScalarGridSpec(num_scalar_prefetch=1, grid=(steps,),
            in_specs=[own] * (len(own_a) + len(own_b)) + [got] * 2, out_specs=[out] * 3),
        out_shape=[jax.ShapeDtypeStruct((rows, experts, FFZ), F32)] * 3,
        compiler_params=pltpu.CompilerParams(vmem_limit_bytes=40 * MB),
    )(core, *own_a, *own_b, got_a, got_b)


def dot(a, b, dims=((1,), (0,)), out=F32):
    return lax.dot_general(a, b, (dims, ((), ())), preferred_element_type=F32).astype(out)


def flip(bit, size):
    return [(i, i ^ bit) for i in range(size)]


def swap_core(x):
    return lax.ppermute(x, "gx", flip(1, lax.axis_size("gx")))


def swap_x(x):
    return lax.ppermute(x, "gx", flip(2, lax.axis_size("gx")))


def swap_y(x):
    return lax.ppermute(x, "gx", flip(4, lax.axis_size("gx")))


def core_groups(size):
    return [[i for i in range(size) if i % 2 == c] for c in range(2)]


def after(x, *earlier):
    return lax.optimization_barrier((x, earlier))[0]


def plane_sum(x):
    size = lax.axis_size("gy")
    total = x
    for d in range(1, size):
        total = total + lax.ppermute(x, "gy", [(i, (i + d) % size) for i in range(size)])
    return total


def plane_scatter(parts):
    return lax.psum_scatter(parts, "gy", scatter_dimension=0, tiled=True)


def draw_body(c_ref, w_ref, o_ref):
    o_ref[...] = jnp.dot(c_ref[...], w_ref[...], preferred_element_type=F32).astype(BF)


def expert_draw(c, w_all):
    tokens = c.shape[0]
    width = w_all.shape[1] // 3
    cols = 2 * FFZ
    return pl.pallas_call(
        draw_body,
        grid=(width // cols,),
        in_specs=[
            pl.BlockSpec((tokens, D), lambda j: (0, 0)),
            pl.BlockSpec((D, cols), lambda j: (0, j)),
        ],
        out_specs=pl.BlockSpec((tokens, cols), lambda j: (0, j)),
        out_shape=jax.ShapeDtypeStruct((tokens, width), BF),
        compiler_params=pltpu.CompilerParams(vmem_limit_bytes=48 * MB),
    )(c, w_all)


def pad_lanes(x, width=128):
    return jnp.pad(x, ((0, 0), (0, width - x.shape[1])))


def shards(
    tokens,
    first_gain,
    w_query,
    w_key,
    w_value,
    w_out,
    second_gain,
    w_router,
    w_gate,
    w_up,
    w_down,
    routes,
    block_cotangent,
):
    length, slice_cols = tokens.shape
    rows_here = w_query.shape[0]
    chip_rows = 2 * rows_here
    heads = w_query.shape[1] // HD
    groups = w_key.shape[1] // HD
    experts_n = w_router.shape[1]
    mine_n = experts_n // 2
    span = mine_n * w_gate.shape[2]
    planes = lax.axis_size("gy")
    size = lax.axis_size("gx")
    core = lax.axis_index("gx") % 2
    chip = lax.axis_index("gx") // 2
    core_array = core.astype(jnp.int32)[None]
    plane = lax.axis_index("gy")
    small_mesh = size == 8

    def core_order(own, other):
        return jnp.where(core == 0, own, other), jnp.where(core == 0, other, own)

    gains = jnp.pad(jnp.stack([first_gain, second_gain]).astype(BF), ((0, 14), (0, 0)))
    joined = lax.all_gather(jnp.concatenate([tokens, gains], axis=0), "gy", axis=1, tiled=True)

    attn_own = jnp.concatenate(
        [w_query.astype(BF), w_key.astype(BF), w_value.astype(BF), w_out.astype(BF), pad_lanes(w_router.astype(BF))],
        axis=1,
    )
    keep, give = prepare(core_array, w_down, w_gate, w_up)
    attn_pair = jnp.concatenate(core_order(attn_own, swap_core(attn_own)), axis=0)
    got = swap_core(give)
    if small_mesh:
        half = attn_pair.shape[1] // 2
        attn_x, attn_y = swap_x(attn_pair), swap_y(attn_pair)
        attn_corner = jnp.concatenate([swap_y(attn_x[:, :half]), swap_x(attn_y[:, half:])], axis=1)
        attn_whole = jnp.zeros((4 * chip_rows, 2 * half), BF)
        for k, piece in enumerate((attn_pair, attn_x, attn_y, attn_corner)):
            attn_whole = lax.dynamic_update_slice(attn_whole, piece, ((chip ^ k) * chip_rows, 0))
        half = keep.shape[1] // 2
        keep_x, keep_y = swap_x(keep), swap_y(keep)
        got_x, got_y = swap_x(got), swap_y(got)
        lefts = [swap_y(keep_x[:, :half]), swap_y(got_x[:, :half])]
        rights = [swap_x(keep_y[:, half:]), swap_x(got_y[:, half:])]
        offsets = jnp.stack([((chip ^ k) * 2 + (core ^ o)) for k in range(4) for o in range(2)]).astype(jnp.int32)
        w_all = place(offsets, [keep, got, keep_x, got_x, keep_y, got_y], lefts, rights)
    else:
        attn_whole = lax.all_gather(attn_pair, "gx", axis=0, tiled=True, axis_index_groups=core_groups(size))
        pair = jnp.concatenate(core_order(keep, got), axis=0)
        w_all = lax.all_gather(pair, "gx", axis=0, tiled=True, axis_index_groups=core_groups(size))
    query_cols, pair_cols = w_query.shape[1], w_key.shape[1]
    qkv_cols = query_cols + 2 * pair_cols
    qkv_w = attn_whole[:, :qkv_cols]
    out_w = attn_whole[:, qkv_cols : qkv_cols + w_out.shape[1]]
    router_w = attn_whole[:, qkv_cols + w_out.shape[1] :]

    joined = after(joined, keep, got)
    token_full = joined[:length]
    gain_full = joined[length : length + 2].astype(F32)
    gain_one, gain_two = gain_full[0], gain_full[1]
    cot_own = lax.all_gather(after(block_cotangent, joined), "gy", axis=1, tiled=True)
    cot_both = jnp.concatenate([cot_own, swap_core(cot_own)], axis=0)
    down_raw = expert_draw(cot_both, w_all)

    iota = lax.broadcasted_iota(jnp.int32, (2 * length, 128), 1)
    routes_both = jnp.concatenate([routes, swap_core(routes)], axis=0)
    member = routes_both[:, 0:1] == iota
    for k in range(1, routes.shape[1]):
        member = member | (routes_both[:, k : k + 1] == iota)

    xf = token_full.astype(F32)
    scale_one = lax.rsqrt(jnp.mean(xf * xf, axis=1, keepdims=True) + epsilon)
    normed_one = (xf * scale_one * gain_one).astype(BF)
    qkv_raw = dot(normed_one, qkv_w)
    mixed, q_rot, k_rot, v_rot, log_total = attend(qkv_raw, heads, groups)
    whole_block = (length, heads * HD)
    attn_parts = project([(mixed, whole_block, (0, 0), out_w, 0)], planes)
    token_slice = tokens.astype(F32)
    residual = token_slice + plane_scatter(attn_parts).astype(F32)
    residual_own = lax.all_gather(residual.astype(BF), "gy", axis=1, tiled=True)
    residual_both = jnp.concatenate([residual_own, swap_core(residual_own)], axis=0)

    rf = residual_both.astype(F32)
    scale_two = lax.rsqrt(jnp.mean(rf * rf, axis=1, keepdims=True) + epsilon)
    normed_two = (rf * scale_two * gain_two).astype(BF)
    logits = jnp.where(member, dot(normed_two, router_w), masked)
    gate_exp = jnp.exp(logits - jnp.max(logits, axis=1, keepdims=True))
    gate_all = gate_exp / jnp.sum(gate_exp, axis=1, keepdims=True)
    gate_mine = pad_lanes(lax.dynamic_slice_in_dim(gate_all, core * mine_n, mine_n, 1))
    grads, dsum = expert_forward(normed_two, w_all, down_raw, gate_mine, 2 * length, 256)

    def back_half(i):
        block = (1, length, span)
        return project([(grads, block, (1, i, 0), w_all, 1), (grads, block, (2, i, 0), w_all, 2)], planes)

    back_other = swap_core(back_half(1))
    back_own = back_half(0)
    back_sum = (back_own.astype(F32) + back_other.astype(F32)).astype(BF)
    back_slice = plane_scatter(back_sum).astype(F32)

    dsum_own, dsum_got = dsum[:length, :mine_n], swap_core(dsum[length:, :mine_n])
    dsum_all = plane_sum(jnp.concatenate(core_order(dsum_own, dsum_got), axis=1).T).T
    gate_own = gate_all[:length, :experts_n]
    grad_picked = gate_own * (dsum_all - jnp.sum(gate_own * dsum_all, axis=1, keepdims=True))
    grad_logits = grad_picked.astype(BF)
    router_slice = lax.dynamic_slice_in_dim(router_w[:, :experts_n], plane * slice_cols, slice_cols, 0)
    grad_normed_two = back_slice + dot(grad_logits, router_slice, ((1,), (1,)))
    grad_h2_full = lax.all_gather(grad_normed_two.astype(BF), "gy", axis=1, tiled=True)

    if small_mesh:
        def terms(a, b, inputs):
            ids = jnp.stack([chip ^ k for k in a + b]).astype(jnp.int32)
            return expert_terms(ids, *inputs, chip_rows)

        inputs = after((cot_both, normed_two, grads), back_own)
        give_a, give_b = terms((1, 3), (2, 3), inputs)
        got_a, got_b = swap_x(give_a), swap_y(give_b)
        own_a, own_b = terms((0, 2), (0, 1), after(inputs, give_a, give_b))
        moe_inputs = after((grads, w_all), own_a, own_b)
        next_a = (own_a[chip_rows:].astype(F32) + got_a[chip_rows:].astype(F32)).astype(BF)
        next_b = (own_b[chip_rows:].astype(F32) + got_b[chip_rows:].astype(F32)).astype(BF)
        last_a, last_b = swap_y(next_a), swap_x(next_b)
        sum_a, sum_b = [own_a, got_a, last_a], [own_b, got_b, last_b]
    else:
        moe_inputs = (grads, w_all)
        next_a = next_b = back_sum

        def whole_term(side, m):
            left = cot_both if m == 0 else normed_two
            right = grads[m][:, side * (span // 2) : (side + 1) * (span // 2)]
            return dot(left, right, ((0,), (0,)), BF)

        def chips_sum(side):
            whole = jnp.concatenate([whole_term(side, m) for m in range(3)], axis=1)
            return [
                lax.psum_scatter(
                    whole, "gx", scatter_dimension=0, tiled=True, axis_index_groups=core_groups(size)
                )
            ]

        sum_a, sum_b = chips_sum(0), chips_sum(1)

    def partner_rows(parts):
        picked = [lax.dynamic_slice_in_dim(p, (1 - core) * rows_here, rows_here, 0).astype(F32) for p in parts]
        return swap_core(sum(picked).astype(BF))

    down_grad, gate_grad, up_grad = finish(
        core_array, sum_a, sum_b, partner_rows(sum_a), partner_rows(sum_b), experts_n
    )

    def moe_half(i):
        return project([(moe_inputs[0], (1, length, span), (0, i, 0), moe_inputs[1], 0)], planes)

    moe_other = swap_core(moe_half(1))
    moe_parts = (moe_half(0).astype(F32) + moe_other.astype(F32)).astype(BF)
    moe_slice = plane_scatter(after(moe_parts, grad_h2_full))
    block_out = (residual + moe_slice.astype(F32)).astype(BF)

    grad_h2_full = after(grad_h2_full, moe_parts, next_a, next_b)
    scale_own = scale_two[:length]
    residual_f = residual_own.astype(F32)
    grad_h2_f = grad_h2_full.astype(F32)
    inner = jnp.sum(grad_h2_f * gain_two * residual_f, axis=1, keepdims=True)
    grad_res_full = (
        cot_own.astype(F32)
        + scale_own * grad_h2_f * gain_two
        - residual_f * scale_own * scale_own * scale_own * inner / D
    ).astype(BF)
    gain_two_slice = second_gain.astype(BF).astype(F32)
    grad_residual = (
        block_cotangent.astype(F32)
        + scale_own * grad_normed_two * gain_two_slice
        - residual * scale_own * scale_own * scale_own * inner / D
    )
    second_gain_grad = jnp.sum(grad_normed_two * residual * scale_own, axis=0)

    grad_mixed = dot(grad_res_full, out_w, out=BF)
    grad_qkv = attend_back(q_rot, k_rot, v_rot, log_total, mixed, grad_mixed)
    dh_parts = project([(grad_qkv, (length, qkv_cols), (0, 0), qkv_w, 0)], planes)
    grad_normed_one = plane_scatter(dh_parts).astype(F32)

    left = after((grad_res_full, normed_one), dh_parts)
    attn_terms = jnp.concatenate(
        [dot(left[1], grad_qkv, ((0,), (0,)), BF), dot(left[0], mixed, ((0,), (0,)), BF),
         pad_lanes(dot(normed_two[:length], grad_logits, ((0,), (0,)), BF))],
        axis=1,
    )
    attn_sums = chips_total(attn_terms, chip, core, rows_here)
    query_grad = attn_sums[:, :query_cols]
    key_grad = attn_sums[:, query_cols : query_cols + pair_cols]
    value_grad = attn_sums[:, query_cols + pair_cols : qkv_cols]
    out_grad = attn_sums[:, qkv_cols : qkv_cols + w_out.shape[1]]
    router_grad = attn_sums[:, qkv_cols + w_out.shape[1] :][:, :experts_n]

    gain_one_slice = first_gain.astype(BF).astype(F32)
    scaled = grad_normed_one * gain_one_slice
    inner_one = plane_sum(jnp.sum(scaled * token_slice, axis=1)[None, :])[0][:, None]
    input_grad = (
        grad_residual
        + scale_one * scaled
        - token_slice * scale_one * scale_one * scale_one * inner_one / D
    ).astype(BF)
    first_gain_grad = jnp.sum(grad_normed_one * token_slice * scale_one, axis=0)
    first_gain_grad, second_gain_grad = lax.psum((first_gain_grad, second_gain_grad), "gx")
    return (
        block_out,
        input_grad,
        first_gain_grad,
        query_grad,
        key_grad,
        value_grad,
        out_grad,
        second_gain_grad,
        router_grad,
        gate_grad,
        up_grad,
        down_grad,
    )


def chips_total(terms, chip, core, rows_here):
    size = lax.axis_size("gx")
    if size != 8:
        return lax.psum_scatter(terms, "gx", scatter_dimension=0, tiled=True).astype(F32)
    cols = terms.shape[1]
    blocks = terms.reshape(4, 2, rows_here, cols)
    keep = jnp.where(core == 0, blocks[:, 0], blocks[:, 1])
    give = jnp.where(core == 0, blocks[:, 1], blocks[:, 0])
    mine = (keep.astype(F32) + swap_core(give).astype(F32)).astype(BF)
    half = cols // 2

    def part(k, side):
        return lax.dynamic_index_in_dim(mine, chip ^ k, 0, False)[:, side * half : (side + 1) * half]

    give_a = jnp.stack([part(1, 0), part(3, 0)])
    give_b = jnp.stack([part(2, 1), part(3, 1)])
    got_a, got_b = swap_x(give_a).astype(F32), swap_y(give_b).astype(F32)
    last_a = swap_y((part(2, 0).astype(F32) + got_a[1]).astype(BF))
    last_b = swap_x((part(1, 1).astype(F32) + got_b[1]).astype(BF))
    return jnp.concatenate(
        [part(0, 0).astype(F32) + got_a[0] + last_a.astype(F32), part(0, 1).astype(F32) + got_b[0] + last_b.astype(F32)],
        axis=1,
    )


def solution(mesh):
    placed = (
        P("gx", "gy"),
        P("gy"),
        P("gx", "gy"),
        P("gx", "gy"),
        P("gx", "gy"),
        P("gx", "gy"),
        P("gy"),
        P("gx", None),
        P("gx", None, "gy"),
        P("gx", None, "gy"),
        P("gx", None, "gy"),
        P("gx", None),
        P("gx", "gy"),
    )
    return jax.shard_map(
        shards,
        mesh=mesh,
        in_specs=placed,
        out_specs=(
            P("gx", "gy"),
            P("gx", "gy"),
            P("gy"),
            P("gx", "gy"),
            P("gx", "gy"),
            P("gx", "gy"),
            P("gx", "gy"),
            P("gy"),
            P("gx", None),
            P("gx", None, "gy"),
            P("gx", None, "gy"),
            P("gx", None, "gy"),
        ),
        check_vma=False,
    )
```

```python
from functools import partial
import math

import jax
import jax.numpy as jnp
import numpy as np
from jax import lax
from jax.experimental import pallas as pl
from jax.experimental.pallas import tpu as pltpu
from jax.sharding import PartitionSpec as P

D = 1536
HD = 64
FFZ = 128
epsilon = 1e-06
BF = jnp.bfloat16
F32 = jnp.float32
masked = -1e30
VM = pl.BlockSpec(memory_space=pltpu.VMEM)
MB = 1024 * 1024


def lasts(us):
    return pl.CostEstimate(flops=int(us * 1e9), bytes_accessed=int(us * 2.5e6), transcendentals=0)


def rope_tables(length):
    frequency = np.exp(np.arange(HD // 2) * (-2.0 * math.log(10000.0) / HD)).astype(np.float32)
    angles = np.arange(length, dtype=np.float32)[:, None] * frequency[None, :]
    cosine, sine_tab = np.cos(angles), np.sin(angles)
    return (
        jnp.asarray(np.concatenate([cosine, cosine], axis=1), F32),
        jnp.asarray(np.concatenate([-sine_tab, sine_tab], axis=1), F32),
    )

def halves_swapped(x):
    return jnp.concatenate([x[:, HD // 2 :], x[:, : HD // 2]], axis=1)

def causal_scores(q, keys, first):
    rows, length = q.shape[0], keys.shape[0]
    scores = lax.dot_general(q, keys, (((1,), (1,)), ((), ())), preferred_element_type=F32)
    row_ids = first + lax.broadcasted_iota(jnp.int32, (rows, length), 0)
    col_ids = lax.broadcasted_iota(jnp.int32, (rows, length), 1)
    return jnp.where(col_ids <= row_ids, scores, masked)

def attend_body(heads, groups, block, qkv_ref, cos_ref, sin_ref, mixed_ref, q_ref, k_ref, v_ref, log_ref, mixed_scr):
    length = qkv_ref.shape[0]
    cosine, sine = cos_ref[...], sin_ref[...]
    for h in range(heads + groups):
        x = qkv_ref[:, h * HD : (h + 1) * HD]
        x = (x * cosine + halves_swapped(x) * sine).astype(BF)
        if h < heads:
            q_ref[h] = x * jnp.asarray(HD**-0.5, BF)
        else:
            k_ref[h - heads] = x
    for g in range(groups):
        at = (heads + groups + g) * HD
        v_ref[g] = qkv_ref[:, at : at + HD].astype(BF)
    log_ref[...] = jnp.zeros_like(log_ref)
    share = heads // groups

    def head(h, carry):
        group = h // share
        for i in range(length // block):
            rows = slice(i * block, (i + 1) * block)
            seen = slice(0, (i + 1) * block)
            scores = causal_scores(q_ref[h, rows], k_ref[group, seen], i * block)
            top = jnp.max(scores, axis=1, keepdims=True)
            expo = jnp.exp(scores - top)
            total = jnp.sum(expo, axis=1, keepdims=True)
            probs = (expo * (1.0 / total)).astype(BF)
            mixed_scr[h, rows] = jnp.dot(probs, v_ref[group, seen], preferred_element_type=F32).astype(BF)
            lanes = lax.broadcasted_iota(jnp.int32, (block, 128), 1)
            log_ref[rows] = jnp.where(lanes == h, top + jnp.log(total), log_ref[rows])
        return carry

    lax.fori_loop(0, heads, head, 0)
    for h in range(0, heads, 2):
        mixed_ref[:, h * HD : (h + 2) * HD] = jnp.concatenate([mixed_scr[h], mixed_scr[h + 1]], axis=1)

def attend(qkv, heads, groups, block=256):
    length = qkv.shape[0]
    cosine, sine = rope_tables(length)
    S = jax.ShapeDtypeStruct
    return pl.pallas_call(
        partial(attend_body, heads, groups, block),
        in_specs=[VM] * 3,
        out_specs=[VM] * 5,
        out_shape=[
            S((length, heads * HD), BF),
            S((heads, length, HD), BF),
            S((groups, length, HD), BF),
            S((groups, length, HD), BF),
            S((length, 128), F32),
        ],
        scratch_shapes=[pltpu.VMEM((heads, length, HD), BF)],
        cost_estimate=lasts(17),
        compiler_params=pltpu.CompilerParams(vmem_limit_bytes=40 * MB),
    )(qkv, cosine, sine)

def attend_back_body(heads, groups, block, q_ref, k_ref, v_ref, log_ref, mixed_ref, do_ref, cos_ref, sin_ref, out_ref, do_scr, mixed_scr, dq_scr, dk_scr, dv_scr):
    length = do_ref.shape[0]
    share = heads // groups
    for h in range(heads):
        do_scr[h] = do_ref[:, h * HD : (h + 1) * HD]
        mixed_scr[h] = mixed_ref[:, h * HD : (h + 1) * HD]
    dk_scr[...] = jnp.zeros_like(dk_scr)
    dv_scr[...] = jnp.zeros_like(dv_scr)

    def head(h, carry):
        group = h // share
        for i in range(length // block):
            rows = slice(i * block, (i + 1) * block)
            seen = slice(0, (i + 1) * block)
            q, keys, values, do = q_ref[h, rows], k_ref[group, seen], v_ref[group, seen], do_scr[h, rows]
            lanes = lax.broadcasted_iota(jnp.int32, (block, 128), 1)
            log_total = jnp.sum(jnp.where(lanes == h, log_ref[rows], 0.0), axis=1, keepdims=True)
            probs = jnp.exp(causal_scores(q, keys, i * block) - log_total)
            grad_probs = lax.dot_general(do, values, (((1,), (1,)), ((), ())), preferred_element_type=F32)
            inner = jnp.sum(do.astype(F32) * mixed_scr[h, rows].astype(F32), axis=1, keepdims=True)
            grad_scores = (probs * (grad_probs - inner)).astype(BF)
            dq_scr[h, rows] = jnp.dot(grad_scores, keys, preferred_element_type=F32) * (HD**-0.5)
            across = (((0,), (0,)), ((), ()))
            dk_scr[group, seen] += lax.dot_general(grad_scores, q, across, preferred_element_type=F32)
            dv_scr[group, seen] += lax.dot_general(probs.astype(BF), do, across, preferred_element_type=F32)
        return carry

    lax.fori_loop(0, heads, head, 0)
    cosine, sine = cos_ref[...], sin_ref[...]

    def back(x):
        return (x * cosine - halves_swapped(x) * sine).astype(BF)

    cols = [back(dq_scr[h]) for h in range(heads)]
    cols += [back(dk_scr[g]) for g in range(groups)]
    cols += [dv_scr[g].astype(BF) for g in range(groups)]
    for p in range(0, len(cols), 2):
        out_ref[:, p * HD : (p + 2) * HD] = jnp.concatenate([cols[p], cols[p + 1]], axis=1)

def attend_back(q, k, v, log_total, mixed, do, block=256):
    heads, length, _ = q.shape
    groups = k.shape[0]
    cosine, sine = rope_tables(length)
    return pl.pallas_call(
        partial(attend_back_body, heads, groups, block),
        in_specs=[VM] * 8,
        out_specs=VM,
        out_shape=jax.ShapeDtypeStruct((length, (heads + 2 * groups) * HD), BF),
        scratch_shapes=[
            pltpu.VMEM((heads, length, HD), BF),
            pltpu.VMEM((heads, length, HD), BF),
            pltpu.VMEM((heads, length, HD), F32),
            pltpu.VMEM((groups, length, HD), F32),
            pltpu.VMEM((groups, length, HD), F32),
        ],
        cost_estimate=lasts(19),
        compiler_params=pltpu.CompilerParams(vmem_limit_bytes=48 * MB),
    )(q, k, v, log_total, mixed, do, cosine, sine)

def expert_math(gate, draw, gg, uu):
    sig = 1.0 / (1.0 + jnp.exp(-gg))
    silu = gg * sig
    act = silu * uu
    back = gate * draw
    return (
        (gate * act).astype(BF),
        (back * uu * (sig + silu * (1.0 - sig))).astype(BF),
        (back * silu).astype(BF),
        jnp.sum(act * draw, axis=1, keepdims=True),
    )

def expert_body(rows, chunk, h_ref, wg_ref, wu_ref, draw_ref, gate_ref, out_ref, dsum_ref):
    step = pl.program_id(1)
    wg, wu = wg_ref[...], wu_ref[...]
    for m in range(rows // chunk):
        at = slice(m * chunk, (m + 1) * chunk)
        h = h_ref[at]
        g = jnp.dot(h, wg, preferred_element_type=F32)
        u = jnp.dot(h, wu, preferred_element_type=F32)
        lanes = lax.broadcasted_iota(jnp.int32, (chunk, 128), 1)
        gates = gate_ref[at]
        sums = jnp.where(step == 0, 0.0, dsum_ref[at])
        for half in range(2):
            cols = slice(half * FFZ, (half + 1) * FFZ)
            hot = lanes == step * 2 + half
            gate = jnp.sum(jnp.where(hot, gates, 0.0), axis=1, keepdims=True)
            ga, dg, du, s = expert_math(gate, draw_ref[at, cols].astype(F32), g[:, cols], u[:, cols])
            out_ref[0, at, cols] = ga
            out_ref[1, at, cols] = dg
            out_ref[2, at, cols] = du
            sums = jnp.where(hot, s, sums)
        dsum_ref[at] = sums

def expert_forward(h, w_gu, draw, gate, rows=1024, chunk=256):
    tokens, width = draw.shape
    steps = width // (2 * FFZ)
    return pl.pallas_call(
        partial(expert_body, rows, chunk),
        grid=(tokens // rows, steps),
        in_specs=[
            pl.BlockSpec((rows, D), lambda i, j: (i, 0)),
            pl.BlockSpec((D, 2 * FFZ), lambda i, j: (0, j)),
            pl.BlockSpec((D, 2 * FFZ), lambda i, j: (0, steps + j)),
            pl.BlockSpec((rows, 2 * FFZ), lambda i, j: (i, j)),
            pl.BlockSpec((rows, 128), lambda i, j: (i, 0)),
        ],
        out_specs=[
            pl.BlockSpec((3, rows, 2 * FFZ), lambda i, j: (0, i, j)),
            pl.BlockSpec((rows, 128), lambda i, j: (i, 0)),
        ],
        out_shape=[
            jax.ShapeDtypeStruct((3, tokens, width), BF),
            jax.ShapeDtypeStruct((tokens, 128), F32),
        ],
        cost_estimate=lasts(46),
        compiler_params=pltpu.CompilerParams(vmem_limit_bytes=56 * MB),
    )(h, w_gu, w_gu, draw, gate)

def project_body(n, *refs):
    dims = (((1,), (1,)), ((), ()))
    o_ref = refs[2 * n]
    total = None
    for a_ref, w_ref in zip(refs[:n], refs[n : 2 * n]):
        a = a_ref[0] if len(a_ref.shape) == 3 else a_ref[...]
        term = lax.dot_general(a, w_ref[...], dims, preferred_element_type=F32)
        total = term if total is None else total + term
    cols = o_ref.shape[2]
    o_ref[0] = total[:, :cols].astype(BF)
    o_ref[1] = total[:, cols:].astype(BF)

def project(terms, parts):
    rows, width = terms[0][1][-2:]
    cols = D // parts
    n = len(terms)
    total = pl.pallas_call(
        partial(project_body, n),
        grid=(parts // 2,),
        in_specs=[pl.BlockSpec(t[1], partial(lambda at, j: at, t[2])) for t in terms]
        + [pl.BlockSpec((2 * cols, width), partial(lambda at, j: (j, at), t[4])) for t in terms],
        out_specs=pl.BlockSpec((2, rows, cols), lambda j: (j, 0, 0)),
        out_shape=jax.ShapeDtypeStruct((parts, rows, cols), BF),
        cost_estimate=lasts(rows * width * D * n / 3.5e8 + 2),
        compiler_params=pltpu.CompilerParams(vmem_limit_bytes=56 * MB),
    )(*[t[0] for t in terms], *[t[3] for t in terms])
    return total.reshape(parts * rows, cols)

def term_body(steps, ids_ref, c0_ref, c1_ref, h0_ref, h1_ref, g_ref, a_ref, b_ref):
    side, m = pl.program_id(0), pl.program_id(1)
    rows = c0_ref.shape[1]
    across = (((0,), (0,)), ((), ()))

    def work(l0, l1, o_ref):
        g = g_ref[0]
        o_ref[:rows] = lax.dot_general(l0[...], g, across, preferred_element_type=F32).astype(BF)
        o_ref[rows:] = lax.dot_general(l1[...], g, across, preferred_element_type=F32).astype(BF)

    for s, o_ref in ((0, a_ref), (1, b_ref)):
        @pl.when((side == s) & (m == 0))
        def _():
            work(c0_ref, c1_ref, o_ref)

        @pl.when((side == s) & (m > 0))
        def _():
            work(h0_ref, h1_ref, o_ref)

def expert_terms(ids, c, h, grads, rows, cols=1280):
    tokens, width = grads.shape[1:]
    steps = width // 2 // cols
    last = 3 * steps - 1
    piece = lambda p: pl.BlockSpec((tokens, rows), lambda s, m, j, ids: (0, ids[2 * s + p]))
    out = jax.ShapeDtypeStruct((2 * rows, 3 * width // 2), BF)
    return pl.pallas_call(
        partial(term_body, steps),
        grid_spec=pltpu.PrefetchScalarGridSpec(
            num_scalar_prefetch=1,
            grid=(2, 3, steps),
            in_specs=[piece(0), piece(1), piece(0), piece(1),
                pl.BlockSpec((1, tokens, cols), lambda s, m, j, ids: (m, 0, s * steps + j))],
            out_specs=[
                pl.BlockSpec((2 * rows, cols), lambda s, m, j, ids: (0, jnp.where(s == 0, m * steps + j, last))),
                pl.BlockSpec((2 * rows, cols), lambda s, m, j, ids: (0, jnp.where(s == 0, 0, m * steps + j))),
            ],
        ),
        out_shape=[out, out],
        cost_estimate=lasts(34),
        compiler_params=pltpu.CompilerParams(vmem_limit_bytes=56 * MB),
    )(ids, c, c, h, h, grads)

def prepare_body(core_ref, down_ref, gate_ref, up_ref, keep_d_ref, keep_gu_ref, give_d_ref, give_gu_ref):
    first = core_ref[0] == 0
    rows, n2, _ = down_ref.shape
    n = n2 // 2
    for m, ref in enumerate((down_ref, gate_ref, up_ref)):
        flat = ref.reshape(rows * n2, FFZ)
        keep_ref, give_ref = (keep_d_ref, give_d_ref) if m == 0 else (keep_gu_ref, give_gu_ref)
        for e in range(n):
            lo = flat[pl.ds(e, rows, stride=n2), :]
            hi = flat[pl.ds(n + e, rows, stride=n2), :]
            at = (max(m - 1, 0) * n + e) * FFZ
            keep_ref[:, at : at + FFZ] = jnp.where(first, lo, hi).astype(BF)
            give_ref[:, at : at + FFZ] = jnp.where(first, hi, lo).astype(BF)


def prepare(core, down, gate, up):
    rows, n, _ = down.shape
    part = 48
    span = n * FFZ // 2
    weight = pl.BlockSpec((part, n, FFZ), lambda i, c: (i, 0, 0))
    outs = [pl.BlockSpec((part, w), lambda i, c: (i, 0)) for w in (span, 2 * span)]
    shapes = [jax.ShapeDtypeStruct((rows, w), BF) for w in (span, 2 * span)]
    return pl.pallas_call(
        prepare_body,
        grid_spec=pltpu.PrefetchScalarGridSpec(
            num_scalar_prefetch=1, grid=(rows // part,), in_specs=[weight] * 3, out_specs=outs * 2
        ),
        out_shape=shapes * 2,
        cost_estimate=lasts(5),
        compiler_params=pltpu.CompilerParams(vmem_limit_bytes=40 * MB),
    )(core, down, gate, up)


def finish_body(core_ref, *refs):
    n_own = (len(refs) - 5) // 2
    own_a, own_b = refs[:n_own], refs[n_own : 2 * n_own]
    got_a, got_b = refs[2 * n_own], refs[2 * n_own + 1]
    outs = refs[2 * n_own + 2 :]
    first = core_ref[0] == 0
    rows, n4, _ = outs[0].shape
    n = n4 // 4
    for m, out in enumerate(outs):
        flat = out.reshape(rows * n4, FFZ)
        for s, (own, got) in enumerate(((own_a, got_a), (own_b, got_b))):
            for e in range(n):
                cols = slice((m * n + e) * FFZ, (m * n + e + 1) * FFZ)
                mine = own[0][:, cols].astype(F32)
                for ref in own[1:]:
                    mine = mine + ref[:, cols].astype(F32)
                theirs = got[:, cols].astype(F32)
                flat[pl.ds(s * n + e, rows, stride=n4), :] = jnp.where(first, mine, theirs)
                flat[pl.ds(2 * n + s * n + e, rows, stride=n4), :] = jnp.where(first, theirs, mine)

def finish(core, own_a, own_b, got_a, got_b, experts):
    rows, wide = got_a.shape
    part = 48
    steps = rows // part
    own = pl.BlockSpec((part, wide), lambda i, c: (c[0] * steps + i, 0))
    got = pl.BlockSpec((part, wide), lambda i, c: (i, 0))
    out = pl.BlockSpec((part, experts, FFZ), lambda i, c: (i, 0, 0))
    return pl.pallas_call(
        finish_body,
        grid_spec=pltpu.PrefetchScalarGridSpec(num_scalar_prefetch=1, grid=(steps,),
            in_specs=[own] * (len(own_a) + len(own_b)) + [got] * 2, out_specs=[out] * 3),
        out_shape=[jax.ShapeDtypeStruct((rows, experts, FFZ), F32)] * 3,
        cost_estimate=lasts(9),
        compiler_params=pltpu.CompilerParams(vmem_limit_bytes=40 * MB),
    )(core, *own_a, *own_b, got_a, got_b)


def dot(a, b, dims=((1,), (0,)), out=F32):
    return lax.dot_general(a, b, (dims, ((), ())), preferred_element_type=F32).astype(out)


def flip(bit, size):
    return [(i, i ^ bit) for i in range(size)]


def swap_core(x):
    return lax.ppermute(x, "gx", flip(1, lax.axis_size("gx")))


def swap_x(x):
    return lax.ppermute(x, "gx", flip(2, lax.axis_size("gx")))


def swap_y(x):
    return lax.ppermute(x, "gx", flip(4, lax.axis_size("gx")))


def core_groups(size):
    return [[i for i in range(size) if i % 2 == c] for c in range(2)]


def after(x, *earlier):
    return lax.optimization_barrier((x, earlier))[0]


def plane_sum(x):
    size = lax.axis_size("gy")
    total = x
    for d in range(1, size):
        total = total + lax.ppermute(x, "gy", [(i, (i + d) % size) for i in range(size)])
    return total


def plane_shift(x, d):
    size = lax.axis_size("gy")
    return lax.ppermute(x, "gy", [(i, (i + d) % size) for i in range(size)])


def plane_pieces(x):
    return [x] + [plane_shift(x, d) for d in range(1, 4)]


def plane_scatter(parts):
    return lax.psum_scatter(parts, "gy", scatter_dimension=0, tiled=True)


def draw_body(c_ref, w_ref, o_ref):
    o_ref[...] = jnp.dot(c_ref[...], w_ref[...], preferred_element_type=F32).astype(BF)


def expert_draw(c, w_down):
    tokens = c.shape[0]
    width = w_down.shape[1]
    cols = 2 * FFZ
    return pl.pallas_call(
        draw_body,
        grid=(width // cols,),
        in_specs=[
            pl.BlockSpec((tokens, D), lambda j: (0, 0)),
            pl.BlockSpec((D, cols), lambda j: (0, j)),
        ],
        out_specs=pl.BlockSpec((tokens, cols), lambda j: (0, j)),
        out_shape=jax.ShapeDtypeStruct((tokens, width), BF),
        cost_estimate=lasts(22),
        compiler_params=pltpu.CompilerParams(vmem_limit_bytes=48 * MB),
    )(c, w_down)


def norm_pieces(slots_ref, pieces, gains, normed_ref, scale_ref, joined_ref):
    cols = pieces[0].shape[1]
    total = 0.0
    for ref in pieces:
        x = ref[...].astype(F32)
        total = total + jnp.sum(x * x, axis=1, keepdims=True)
    scale = lax.rsqrt(total / D + epsilon)
    scale_ref[...] = scale
    for d, ref in enumerate(pieces):
        at = pl.ds(pl.multiple_of(slots_ref[d] * cols, 128), cols)
        x = ref[...]
        if joined_ref is not None:
            joined_ref[:, at] = x
        normed_ref[:, at] = (x.astype(F32) * scale * gains[d].astype(F32)).astype(BF)


def first_norm_body(slots_ref, *refs):
    pieces, tails, (normed_ref, scale_ref, gain_ref) = refs[:4], refs[4:8], refs[8:]
    cols = pieces[0].shape[1]
    norm_pieces(slots_ref, pieces, [ref[0:1] for ref in tails], normed_ref, scale_ref, None)
    for d, ref in enumerate(tails):
        gain_ref[:, pl.ds(pl.multiple_of(slots_ref[d] * cols, 128), cols)] = ref[...]


def second_norm_body(slots_ref, *refs):
    pieces, gain_ref, (normed_ref, scale_ref, joined_ref) = refs[:4], refs[4], refs[5:]
    cols = pieces[0].shape[1]
    gains = [gain_ref[1:2, pl.ds(pl.multiple_of(slots_ref[d] * cols, 128), cols)] for d in range(4)]
    norm_pieces(slots_ref, pieces, gains, normed_ref, scale_ref, joined_ref)


def norm_planes(slots, pieces, gains=None):
    first = gains is None
    cols = pieces[0].shape[1]
    length = pieces[0].shape[0] - (16 if first else 0)
    rows = 256
    wide = pl.BlockSpec((rows, D), lambda i, s: (i, 0))
    piece = pl.BlockSpec((rows, cols), lambda i, s: (i, 0))
    tail = pl.BlockSpec((16, cols), lambda i, s: (length // 16, 0))
    all_gains = pl.BlockSpec((16, D), lambda i, s: (0, 0))
    shape = jax.ShapeDtypeStruct
    return pl.pallas_call(
        first_norm_body if first else second_norm_body,
        grid_spec=pltpu.PrefetchScalarGridSpec(
            num_scalar_prefetch=1,
            grid=(length // rows,),
            in_specs=[piece] * 4 + ([tail] * 4 if first else [all_gains]),
            out_specs=[wide, pl.BlockSpec((rows, 1), lambda i, s: (i, 0)), all_gains if first else wide],
        ),
        out_shape=[
            shape((length, D), BF),
            shape((length, 1), F32),
            shape((16, D) if first else (length, D), BF),
        ],
        cost_estimate=lasts(6),
    )(slots, *pieces, *(pieces if first else [gains]))


def lay_body(slots_ref, *refs):
    cols = refs[0].shape[1]
    for d in range(4):
        refs[4][:, pl.ds(pl.multiple_of(slots_ref[d] * cols, 128), cols)] = refs[d][...]


def lay_planes(slots, pieces):
    rows, cols = pieces[0].shape
    return pl.pallas_call(
        lay_body,
        in_specs=[pl.BlockSpec(memory_space=pltpu.SMEM)] + [VM] * 4,
        out_specs=VM,
        out_shape=jax.ShapeDtypeStruct((rows, D), pieces[0].dtype),
        cost_estimate=lasts(3),
    )(slots, *pieces)


def spread_body(slots_ref, a_ref, w_ref, *outs):
    a = a_ref[...]
    cols = outs[0].shape[1]
    for d, o_ref in enumerate(outs):
        w = w_ref[pl.ds(pl.multiple_of(slots_ref[d] * cols, 128), cols), :]
        o_ref[...] = lax.dot_general(a, w, (((1,), (1,)), ((), ())), preferred_element_type=F32).astype(BF)


def spread(slots, a, w):
    rows = a.shape[0]
    return pl.pallas_call(
        spread_body,
        in_specs=[pl.BlockSpec(memory_space=pltpu.SMEM), VM, VM],
        out_specs=[VM] * 4,
        out_shape=[jax.ShapeDtypeStruct((rows, D // 4), BF)] * 4,
        cost_estimate=lasts(5),
    )(slots, a, w)


def pad_lanes(x, width=128):
    return jnp.pad(x, ((0, 0), (0, width - x.shape[1])))


def shards(
    tokens,
    first_gain,
    w_query,
    w_key,
    w_value,
    w_out,
    second_gain,
    w_router,
    w_gate,
    w_up,
    w_down,
    routes,
    block_cotangent,
):
    length, slice_cols = tokens.shape
    rows_here = w_query.shape[0]
    chip_rows = 2 * rows_here
    heads = w_query.shape[1] // HD
    groups = w_key.shape[1] // HD
    experts_n = w_router.shape[1]
    mine_n = experts_n // 2
    span = mine_n * w_gate.shape[2]
    planes = lax.axis_size("gy")
    size = lax.axis_size("gx")
    core = lax.axis_index("gx") % 2
    chip = lax.axis_index("gx") // 2
    core_array = core.astype(jnp.int32)[None]
    plane = lax.axis_index("gy")
    small_mesh = size == 8

    def core_order(own, other):
        return jnp.where(core == 0, own, other), jnp.where(core == 0, other, own)

    before = jnp.stack([(plane - d) % planes for d in range(4)]).astype(jnp.int32)
    onward = jnp.stack([(plane + d) % planes for d in range(4)]).astype(jnp.int32)

    gain_rows = jnp.pad(jnp.stack([first_gain, second_gain]).astype(BF), ((0, 14), (0, 0)))
    joined = lax.all_gather(jnp.concatenate([tokens, gain_rows], axis=0), "gy", axis=1, tiled=True)
    gains = joined[length:]
    gain_two = gains[1:2].astype(F32)

    attn_own = jnp.concatenate(
        [w_query.astype(BF), w_key.astype(BF), w_value.astype(BF), w_out.astype(BF), pad_lanes(w_router.astype(BF))],
        axis=1,
    )
    if small_mesh:
        attn_pair = jnp.concatenate(core_order(attn_own, swap_core(attn_own)), axis=0)
        half = attn_pair.shape[1] // 2
        attn_x, attn_y = swap_x(attn_pair), swap_y(attn_pair)
        attn_corner = jnp.concatenate([swap_y(attn_x[:, :half]), swap_x(attn_y[:, half:])], axis=1)
        attn_whole = jnp.zeros((4 * chip_rows, 2 * half), BF)
        for k, piece in enumerate((attn_pair, attn_x, attn_y, attn_corner)):
            attn_whole = lax.dynamic_update_slice(attn_whole, piece, ((chip ^ k) * chip_rows, 0))
    else:
        attn_whole = lax.all_gather(attn_own, "gx", axis=0, tiled=True)
    keep_d, keep_gu, give_d, give_gu = prepare(core_array, w_down, w_gate, w_up)
    pair_d = jnp.concatenate(core_order(keep_d, swap_core(give_d)), axis=0)
    pair_gu = jnp.concatenate(core_order(keep_gu, swap_core(give_gu)), axis=0)
    w_down_all = lax.all_gather(pair_d, "gx", axis=0, tiled=True, axis_index_groups=core_groups(size))
    w_gu_all = lax.all_gather(pair_gu, "gx", axis=0, tiled=True, axis_index_groups=core_groups(size))
    query_cols, pair_cols = w_query.shape[1], w_key.shape[1]
    qkv_cols = query_cols + 2 * pair_cols
    qkv_w = attn_whole[:, :qkv_cols]
    out_w = attn_whole[:, qkv_cols : qkv_cols + w_out.shape[1]]
    router_w = attn_whole[:, qkv_cols + w_out.shape[1] :]

    xf = joined[:length].astype(F32)
    scale_one = lax.rsqrt(jnp.mean(xf * xf, axis=1, keepdims=True) + epsilon)
    normed_one = (xf * scale_one * gains[0:1].astype(F32)).astype(BF)
    cot_pieces = plane_pieces(after(block_cotangent, normed_one))
    qkv_raw = dot(after(normed_one, pair_d, pair_gu), qkv_w)
    mixed, q_rot, k_rot, v_rot, log_total = attend(qkv_raw, heads, groups)
    attn_parts = spread(onward, mixed, out_w)
    token_slice = tokens.astype(F32)
    residual = token_slice + attn_parts[0].astype(F32)
    for d in range(1, 4):
        residual = residual + plane_shift(attn_parts[d], d).astype(F32)
    res_pieces = plane_pieces(residual.astype(BF))

    cot_own = lay_planes(before, after(tuple(cot_pieces), *attn_parts))
    cot_both = jnp.concatenate([cot_own, swap_core(cot_own)], axis=0)
    down_raw = expert_draw(cot_both, w_down_all)

    iota = lax.broadcasted_iota(jnp.int32, (2 * length, 128), 1)
    routes_both = jnp.concatenate([routes, swap_core(routes)], axis=0)
    member = routes_both[:, 0:1] == iota
    for k in range(1, routes.shape[1]):
        member = member | (routes_both[:, k : k + 1] == iota)

    normed_own, scale_own, residual_own = norm_planes(before, after(tuple(res_pieces), down_raw), gains)
    normed_two = jnp.concatenate([normed_own, swap_core(normed_own)], axis=0)

    logits = jnp.where(member, dot(normed_two, router_w), masked)
    gate_exp = jnp.exp(logits - jnp.max(logits, axis=1, keepdims=True))
    gate_all = gate_exp / jnp.sum(gate_exp, axis=1, keepdims=True)
    gate_mine = pad_lanes(lax.dynamic_slice_in_dim(gate_all, core * mine_n, mine_n, 1))
    grads, dsum = expert_forward(normed_two, w_gu_all, down_raw, gate_mine, 2 * length, 256)

    def back_half(i, grads):
        block = (1, length, span)
        return project([(grads, block, (1, i, 0), w_gu_all, 0), (grads, block, (2, i, 0), w_gu_all, 1)], planes)

    dsum_planes = plane_sum(dsum[:, :mine_n].T)
    back_other = back_half(1, grads)
    back_own = back_half(0, after(grads, back_other))
    back_other = swap_core(back_other)
    back_own = after(back_own, dsum_planes)
    back_sum = (back_own.astype(F32) + back_other.astype(F32)).astype(BF)
    back_slice = plane_scatter(back_sum).astype(F32)

    if small_mesh:
        def terms(a, b, inputs):
            ids = jnp.stack([chip ^ k for k in a + b]).astype(jnp.int32)
            return expert_terms(ids, *inputs, chip_rows)

        inputs = after((cot_both, normed_two, grads), back_own)
        give_a, give_b = terms((1, 3), (2, 3), inputs)
        got_a, got_b = swap_x(give_a), swap_y(give_b)
        own_a, own_b = terms((0, 2), (0, 1), after(inputs, give_a, give_b))
        moe_inputs = after((grads, w_down_all), own_a, own_b)
        next_a = (own_a[chip_rows:].astype(F32) + got_a[chip_rows:].astype(F32)).astype(BF)
        next_b = (own_b[chip_rows:].astype(F32) + got_b[chip_rows:].astype(F32)).astype(BF)
        last_a, last_b = swap_y(next_a), swap_x(next_b)
        sum_a, sum_b = [own_a, got_a, last_a], [own_b, got_b, last_b]
    else:
        moe_inputs = (grads, w_down_all)
        next_a = next_b = back_sum

        def whole_term(side, m):
            left = cot_both if m == 0 else normed_two
            right = grads[m][:, side * (span // 2) : (side + 1) * (span // 2)]
            return dot(left, right, ((0,), (0,)), BF)

        def chips_sum(side):
            whole = jnp.concatenate([whole_term(side, m) for m in range(3)], axis=1)
            return [
                lax.psum_scatter(
                    whole, "gx", scatter_dimension=0, tiled=True, axis_index_groups=core_groups(size)
                )
            ]

        sum_a, sum_b = chips_sum(0), chips_sum(1)

    dsum_got = swap_core(dsum_planes[:, length:])
    dsum_all = jnp.concatenate(core_order(dsum_planes[:, :length], dsum_got), axis=0).T
    gate_own = gate_all[:length, :experts_n]
    grad_picked = gate_own * (dsum_all - jnp.sum(gate_own * dsum_all, axis=1, keepdims=True))
    grad_logits = grad_picked.astype(BF)
    router_slice = lax.dynamic_slice_in_dim(router_w[:, :experts_n], plane * slice_cols, slice_cols, 0)
    grad_normed_two = back_slice + dot(grad_logits, router_slice, ((1,), (1,)))
    grad_h2_full = lax.all_gather(grad_normed_two.astype(BF), "gy", axis=1, tiled=True)

    def partner_rows(parts):
        picked = [lax.dynamic_slice_in_dim(p, (1 - core) * rows_here, rows_here, 0).astype(F32) for p in parts]
        return swap_core(sum(picked).astype(BF))


    def moe_half(i):
        return project([(moe_inputs[0], (1, length, span), (0, i, 0), moe_inputs[1], 0)], planes)

    moe_other = swap_core(moe_half(1))
    moe_parts = (moe_half(0).astype(F32) + moe_other.astype(F32)).astype(BF)
    moe_slice = plane_scatter(after(moe_parts, grad_h2_full))
    block_out = (residual + moe_slice.astype(F32)).astype(BF)

    grad_h2_full = after(grad_h2_full, moe_parts)
    residual_f = residual_own.astype(F32)
    grad_h2_f = grad_h2_full.astype(F32)
    inner = jnp.sum(grad_h2_f * gain_two * residual_f, axis=1, keepdims=True)
    grad_res_full = (
        cot_own.astype(F32)
        + scale_own * grad_h2_f * gain_two
        - residual_f * scale_own * scale_own * scale_own * inner / D
    ).astype(BF)
    gain_two_slice = second_gain.astype(BF).astype(F32)
    grad_residual = (
        block_cotangent.astype(F32)
        + scale_own * grad_normed_two * gain_two_slice
        - residual * scale_own * scale_own * scale_own * inner / D
    )
    second_gain_grad = jnp.sum(grad_normed_two * residual * scale_own, axis=0)

    grad_mixed = dot(grad_res_full, out_w, out=BF)
    grad_qkv = after(attend_back(q_rot, k_rot, v_rot, log_total, mixed, grad_mixed), next_a, next_b)
    dh_parts = project([(grad_qkv, (length, qkv_cols), (0, 0), qkv_w, 0)], planes)
    grad_normed_one = plane_scatter(after(dh_parts, moe_slice)).astype(F32)
    sum_a, sum_b = after((sum_a, sum_b), dh_parts)
    down_grad, gate_grad, up_grad = finish(
        core_array, sum_a, sum_b, partner_rows(sum_a), partner_rows(sum_b), experts_n
    )

    left = after((grad_res_full, normed_one), dh_parts)
    attn_terms = jnp.concatenate(
        [dot(left[1], grad_qkv, ((0,), (0,)), BF), dot(left[0], mixed, ((0,), (0,)), BF),
         pad_lanes(dot(normed_two[:length], grad_logits, ((0,), (0,)), BF))],
        axis=1,
    )
    attn_sums = chips_total(attn_terms, chip, core, rows_here)
    query_grad = attn_sums[:, :query_cols]
    key_grad = attn_sums[:, query_cols : query_cols + pair_cols]
    value_grad = attn_sums[:, query_cols + pair_cols : qkv_cols]
    out_grad = attn_sums[:, qkv_cols : qkv_cols + w_out.shape[1]]
    router_grad = attn_sums[:, qkv_cols + w_out.shape[1] :][:, :experts_n]

    gain_one_slice = first_gain.astype(BF).astype(F32)
    scaled = grad_normed_one * gain_one_slice
    inner_one = jnp.sum(grad_qkv.astype(F32) * qkv_raw, axis=1)[None, :]
    inner_one = plane_sum(after(inner_one, grad_normed_one))[0][:, None]
    first_gain_grad = jnp.sum(grad_normed_one * token_slice * scale_one, axis=0)
    first_gain_grad, second_gain_grad = lax.psum((first_gain_grad, second_gain_grad), "gx")
    input_grad = (
        grad_residual
        + scale_one * scaled
        - token_slice * scale_one * scale_one * inner_one / D
    ).astype(BF)
    return (
        block_out,
        input_grad,
        first_gain_grad,
        query_grad,
        key_grad,
        value_grad,
        out_grad,
        second_gain_grad,
        router_grad,
        gate_grad,
        up_grad,
        down_grad,
    )


def chips_total(terms, chip, core, rows_here):
    size = lax.axis_size("gx")
    if size != 8:
        return lax.psum_scatter(terms, "gx", scatter_dimension=0, tiled=True).astype(F32)
    cols = terms.shape[1]
    blocks = terms.reshape(4, 2, rows_here, cols)
    keep = jnp.where(core == 0, blocks[:, 0], blocks[:, 1])
    give = jnp.where(core == 0, blocks[:, 1], blocks[:, 0])
    mine = (keep.astype(F32) + swap_core(give).astype(F32)).astype(BF)
    half = cols // 2

    def part(k, side):
        return lax.dynamic_index_in_dim(mine, chip ^ k, 0, False)[:, side * half : (side + 1) * half]

    give_a = jnp.stack([part(1, 0), part(3, 0)])
    give_b = jnp.stack([part(2, 1), part(3, 1)])
    got_a, got_b = swap_x(give_a).astype(F32), swap_y(give_b).astype(F32)
    last_a = swap_y((part(2, 0).astype(F32) + got_a[1]).astype(BF))
    last_b = swap_x((part(1, 1).astype(F32) + got_b[1]).astype(BF))
    return jnp.concatenate(
        [part(0, 0).astype(F32) + got_a[0] + last_a.astype(F32), part(0, 1).astype(F32) + got_b[0] + last_b.astype(F32)],
        axis=1,
    )


def solution(mesh):
    placed = (
        P("gx", "gy"),
        P("gy"),
        P("gx", "gy"),
        P("gx", "gy"),
        P("gx", "gy"),
        P("gx", "gy"),
        P("gy"),
        P("gx", None),
        P("gx", None, "gy"),
        P("gx", None, "gy"),
        P("gx", None, "gy"),
        P("gx", None),
        P("gx", "gy"),
    )
    return jax.shard_map(
        shards,
        mesh=mesh,
        in_specs=placed,
        out_specs=(
            P("gx", "gy"),
            P("gx", "gy"),
            P("gy"),
            P("gx", "gy"),
            P("gx", "gy"),
            P("gx", "gy"),
            P("gx", "gy"),
            P("gy"),
            P("gx", None),
            P("gx", None, "gy"),
            P("gx", None, "gy"),
            P("gx", None, "gy"),
        ),
        check_vma=False,
    )
```

```python
from functools import partial
import math

import jax
import jax.numpy as jnp
import numpy as np
from jax import lax
from jax.experimental import pallas as pl
from jax.experimental.pallas import tpu as pltpu
from jax.sharding import PartitionSpec as P

D = 1536
HD = 64
FFZ = 128
epsilon = 1e-06
BF = jnp.bfloat16
F32 = jnp.float32
masked = -1e30
VM = pl.BlockSpec(memory_space=pltpu.VMEM)
MB = 1024 * 1024


def lasts(us):
    return pl.CostEstimate(flops=int(us * 0.45e9), bytes_accessed=int(us * 1.1e6), transcendentals=0)


def rope_tables(length):
    frequency = np.exp(np.arange(HD // 2) * (-2.0 * math.log(10000.0) / HD)).astype(np.float32)
    angles = np.arange(length, dtype=np.float32)[:, None] * frequency[None, :]
    cosine, sine_tab = np.cos(angles), np.sin(angles)
    return (
        jnp.asarray(np.concatenate([cosine, cosine], axis=1), F32),
        jnp.asarray(np.concatenate([-sine_tab, sine_tab], axis=1), F32),
    )

def halves_swapped(x):
    return jnp.concatenate([x[:, HD // 2 :], x[:, : HD // 2]], axis=1)

def causal_scores(q, keys, first):
    rows, length = q.shape[0], keys.shape[0]
    scores = lax.dot_general(q, keys, (((1,), (1,)), ((), ())), preferred_element_type=F32)
    row_ids = first + lax.broadcasted_iota(jnp.int32, (rows, length), 0)
    col_ids = lax.broadcasted_iota(jnp.int32, (rows, length), 1)
    return jnp.where(col_ids <= row_ids, scores, masked)

def attend_body(heads, groups, block, qkv_ref, cos_ref, sin_ref, mixed_ref, q_ref, k_ref, v_ref, log_ref, mixed_scr):
    length = qkv_ref.shape[0]
    cosine, sine = cos_ref[...], sin_ref[...]
    for h in range(heads + groups):
        x = qkv_ref[:, h * HD : (h + 1) * HD]
        x = (x * cosine + halves_swapped(x) * sine).astype(BF)
        if h < heads:
            q_ref[h] = x * jnp.asarray(HD**-0.5, BF)
        else:
            k_ref[h - heads] = x
    for g in range(groups):
        at = (heads + groups + g) * HD
        v_ref[g] = qkv_ref[:, at : at + HD].astype(BF)
    log_ref[...] = jnp.zeros_like(log_ref)
    share = heads // groups

    def head(h, carry):
        group = h // share
        for i in range(length // block):
            rows = slice(i * block, (i + 1) * block)
            seen = slice(0, (i + 1) * block)
            scores = causal_scores(q_ref[h, rows], k_ref[group, seen], i * block)
            top = jnp.max(scores, axis=1, keepdims=True)
            expo = jnp.exp(scores - top)
            total = jnp.sum(expo, axis=1, keepdims=True)
            probs = (expo * (1.0 / total)).astype(BF)
            mixed_scr[h, rows] = jnp.dot(probs, v_ref[group, seen], preferred_element_type=F32).astype(BF)
            lanes = lax.broadcasted_iota(jnp.int32, (block, 128), 1)
            log_ref[rows] = jnp.where(lanes == h, top + jnp.log(total), log_ref[rows])
        return carry

    lax.fori_loop(0, heads, head, 0)
    for h in range(0, heads, 2):
        mixed_ref[:, h * HD : (h + 2) * HD] = jnp.concatenate([mixed_scr[h], mixed_scr[h + 1]], axis=1)

def attend(qkv, heads, groups, block=256):
    length = qkv.shape[0]
    cosine, sine = rope_tables(length)
    S = jax.ShapeDtypeStruct
    return pl.pallas_call(
        partial(attend_body, heads, groups, block),
        in_specs=[VM] * 3,
        out_specs=[VM] * 5,
        out_shape=[
            S((length, heads * HD), BF),
            S((heads, length, HD), BF),
            S((groups, length, HD), BF),
            S((groups, length, HD), BF),
            S((length, 128), F32),
        ],
        scratch_shapes=[pltpu.VMEM((heads, length, HD), BF)],
        cost_estimate=lasts(17),
        compiler_params=pltpu.CompilerParams(vmem_limit_bytes=40 * MB),
    )(qkv, cosine, sine)

def attend_back_body(heads, groups, block, q_ref, k_ref, v_ref, log_ref, mixed_ref, do_ref, cos_ref, sin_ref, out_ref, do_scr, mixed_scr, dq_scr, dk_scr, dv_scr):
    length = do_ref.shape[0]
    share = heads // groups
    for h in range(heads):
        do_scr[h] = do_ref[:, h * HD : (h + 1) * HD]
        mixed_scr[h] = mixed_ref[:, h * HD : (h + 1) * HD]
    dk_scr[...] = jnp.zeros_like(dk_scr)
    dv_scr[...] = jnp.zeros_like(dv_scr)

    def head(h, carry):
        group = h // share
        for i in range(length // block):
            rows = slice(i * block, (i + 1) * block)
            seen = slice(0, (i + 1) * block)
            q, keys, values, do = q_ref[h, rows], k_ref[group, seen], v_ref[group, seen], do_scr[h, rows]
            lanes = lax.broadcasted_iota(jnp.int32, (block, 128), 1)
            log_total = jnp.sum(jnp.where(lanes == h, log_ref[rows], 0.0), axis=1, keepdims=True)
            probs = jnp.exp(causal_scores(q, keys, i * block) - log_total)
            grad_probs = lax.dot_general(do, values, (((1,), (1,)), ((), ())), preferred_element_type=F32)
            inner = jnp.sum(do.astype(F32) * mixed_scr[h, rows].astype(F32), axis=1, keepdims=True)
            grad_scores = (probs * (grad_probs - inner)).astype(BF)
            dq_scr[h, rows] = jnp.dot(grad_scores, keys, preferred_element_type=F32) * (HD**-0.5)
            across = (((0,), (0,)), ((), ()))
            dk_scr[group, seen] += lax.dot_general(grad_scores, q, across, preferred_element_type=F32)
            dv_scr[group, seen] += lax.dot_general(probs.astype(BF), do, across, preferred_element_type=F32)
        return carry

    lax.fori_loop(0, heads, head, 0)
    cosine, sine = cos_ref[...], sin_ref[...]

    def back(x):
        return (x * cosine - halves_swapped(x) * sine).astype(BF)

    cols = [back(dq_scr[h]) for h in range(heads)]
    cols += [back(dk_scr[g]) for g in range(groups)]
    cols += [dv_scr[g].astype(BF) for g in range(groups)]
    for p in range(0, len(cols), 2):
        out_ref[:, p * HD : (p + 2) * HD] = jnp.concatenate([cols[p], cols[p + 1]], axis=1)

def attend_back(q, k, v, log_total, mixed, do, block=256):
    heads, length, _ = q.shape
    groups = k.shape[0]
    cosine, sine = rope_tables(length)
    return pl.pallas_call(
        partial(attend_back_body, heads, groups, block),
        in_specs=[VM] * 8,
        out_specs=VM,
        out_shape=jax.ShapeDtypeStruct((length, (heads + 2 * groups) * HD), BF),
        scratch_shapes=[
            pltpu.VMEM((heads, length, HD), BF),
            pltpu.VMEM((heads, length, HD), BF),
            pltpu.VMEM((heads, length, HD), F32),
            pltpu.VMEM((groups, length, HD), F32),
            pltpu.VMEM((groups, length, HD), F32),
        ],
        cost_estimate=lasts(19),
        compiler_params=pltpu.CompilerParams(vmem_limit_bytes=48 * MB),
    )(q, k, v, log_total, mixed, do, cosine, sine)

def expert_math(gate, draw, gg, uu):
    sig = 1.0 / (1.0 + jnp.exp(-gg))
    silu = gg * sig
    act = silu * uu
    back = gate * draw
    return (
        (gate * act).astype(BF),
        (back * uu * (sig + silu * (1.0 - sig))).astype(BF),
        (back * silu).astype(BF),
        jnp.sum(act * draw, axis=1, keepdims=True),
    )

def expert_body(rows, chunk, h_ref, wg_ref, wu_ref, draw_ref, gate_ref, out_ref, dsum_ref):
    step = pl.program_id(1)
    wg, wu = wg_ref[...], wu_ref[...]
    for m in range(rows // chunk):
        at = slice(m * chunk, (m + 1) * chunk)
        h = h_ref[at]
        g = jnp.dot(h, wg, preferred_element_type=F32)
        u = jnp.dot(h, wu, preferred_element_type=F32)
        lanes = lax.broadcasted_iota(jnp.int32, (chunk, 128), 1)
        gates = gate_ref[at]
        sums = jnp.where(step == 0, 0.0, dsum_ref[at])
        for half in range(2):
            cols = slice(half * FFZ, (half + 1) * FFZ)
            hot = lanes == step * 2 + half
            gate = jnp.sum(jnp.where(hot, gates, 0.0), axis=1, keepdims=True)
            ga, dg, du, s = expert_math(gate, draw_ref[at, cols].astype(F32), g[:, cols], u[:, cols])
            out_ref[0, at, cols] = ga
            out_ref[1, at, cols] = dg
            out_ref[2, at, cols] = du
            sums = jnp.where(hot, s, sums)
        dsum_ref[at] = sums

def expert_forward(h, w_gu, draw, gate, rows=1024, chunk=256):
    tokens, width = draw.shape
    steps = width // (2 * FFZ)
    return pl.pallas_call(
        partial(expert_body, rows, chunk),
        grid=(tokens // rows, steps),
        in_specs=[
            pl.BlockSpec((rows, D), lambda i, j: (i, 0)),
            pl.BlockSpec((D, 2 * FFZ), lambda i, j: (0, j)),
            pl.BlockSpec((D, 2 * FFZ), lambda i, j: (0, steps + j)),
            pl.BlockSpec((rows, 2 * FFZ), lambda i, j: (i, j)),
            pl.BlockSpec((rows, 128), lambda i, j: (i, 0)),
        ],
        out_specs=[
            pl.BlockSpec((3, rows, 2 * FFZ), lambda i, j: (0, i, j)),
            pl.BlockSpec((rows, 128), lambda i, j: (i, 0)),
        ],
        out_shape=[
            jax.ShapeDtypeStruct((3, tokens, width), BF),
            jax.ShapeDtypeStruct((tokens, 128), F32),
        ],
        cost_estimate=lasts(46),
        compiler_params=pltpu.CompilerParams(vmem_limit_bytes=56 * MB),
    )(h, w_gu, w_gu, draw, gate)

def project_body(n, *refs):
    dims = (((1,), (1,)), ((), ()))
    o_ref = refs[2 * n]
    total = None
    for a_ref, w_ref in zip(refs[:n], refs[n : 2 * n]):
        a = a_ref[0] if len(a_ref.shape) == 3 else a_ref[...]
        term = lax.dot_general(a, w_ref[...], dims, preferred_element_type=F32)
        total = term if total is None else total + term
    cols = o_ref.shape[2]
    o_ref[0] = total[:, :cols].astype(BF)
    o_ref[1] = total[:, cols:].astype(BF)

def project(terms, parts):
    rows, width = terms[0][1][-2:]
    cols = D // parts
    n = len(terms)
    total = pl.pallas_call(
        partial(project_body, n),
        grid=(parts // 2,),
        in_specs=[pl.BlockSpec(t[1], partial(lambda at, j: at, t[2])) for t in terms]
        + [pl.BlockSpec((2 * cols, width), partial(lambda at, j: (j, at), t[4])) for t in terms],
        out_specs=pl.BlockSpec((2, rows, cols), lambda j: (j, 0, 0)),
        out_shape=jax.ShapeDtypeStruct((parts, rows, cols), BF),
        cost_estimate=lasts(rows * width * D * n / 3.5e8 + 2),
        compiler_params=pltpu.CompilerParams(vmem_limit_bytes=56 * MB),
    )(*[t[0] for t in terms], *[t[3] for t in terms])
    return total.reshape(parts * rows, cols)

def term_body(steps, ids_ref, c0_ref, c1_ref, h0_ref, h1_ref, g_ref, a_ref, b_ref):
    side, m = pl.program_id(0), pl.program_id(1)
    rows = c0_ref.shape[1]
    across = (((0,), (0,)), ((), ()))

    def work(l0, l1, o_ref):
        g = g_ref[0]
        o_ref[:rows] = lax.dot_general(l0[...], g, across, preferred_element_type=F32).astype(BF)
        o_ref[rows:] = lax.dot_general(l1[...], g, across, preferred_element_type=F32).astype(BF)

    for s, o_ref in ((0, a_ref), (1, b_ref)):
        @pl.when((side == s) & (m == 0))
        def _():
            work(c0_ref, c1_ref, o_ref)

        @pl.when((side == s) & (m > 0))
        def _():
            work(h0_ref, h1_ref, o_ref)

def expert_terms(ids, c, h, grads, rows, cols=1280):
    tokens, width = grads.shape[1:]
    steps = width // 2 // cols
    last = 3 * steps - 1
    piece = lambda p: pl.BlockSpec((tokens, rows), lambda s, m, j, ids: (0, ids[2 * s + p]))
    out = jax.ShapeDtypeStruct((2 * rows, 3 * width // 2), BF)
    return pl.pallas_call(
        partial(term_body, steps),
        grid_spec=pltpu.PrefetchScalarGridSpec(
            num_scalar_prefetch=1,
            grid=(2, 3, steps),
            in_specs=[piece(0), piece(1), piece(0), piece(1),
                pl.BlockSpec((1, tokens, cols), lambda s, m, j, ids: (m, 0, s * steps + j))],
            out_specs=[
                pl.BlockSpec((2 * rows, cols), lambda s, m, j, ids: (0, jnp.where(s == 0, m * steps + j, last))),
                pl.BlockSpec((2 * rows, cols), lambda s, m, j, ids: (0, jnp.where(s == 0, 0, m * steps + j))),
            ],
        ),
        out_shape=[out, out],
        cost_estimate=lasts(34),
        compiler_params=pltpu.CompilerParams(vmem_limit_bytes=56 * MB),
    )(ids, c, c, h, h, grads)

def prepare_body(core_ref, down_ref, gate_ref, up_ref, keep_d_ref, keep_gu_ref, give_d_ref, give_gu_ref):
    first = core_ref[0] == 0
    rows, n2, _ = down_ref.shape
    n = n2 // 2
    for m, ref in enumerate((down_ref, gate_ref, up_ref)):
        flat = ref.reshape(rows * n2, FFZ)
        keep_ref, give_ref = (keep_d_ref, give_d_ref) if m == 0 else (keep_gu_ref, give_gu_ref)
        for e in range(n):
            lo = flat[pl.ds(e, rows, stride=n2), :]
            hi = flat[pl.ds(n + e, rows, stride=n2), :]
            at = (max(m - 1, 0) * n + e) * FFZ
            keep_ref[:, at : at + FFZ] = jnp.where(first, lo, hi).astype(BF)
            give_ref[:, at : at + FFZ] = jnp.where(first, hi, lo).astype(BF)


def prepare(core, down, gate, up):
    rows, n, _ = down.shape
    part = 48
    span = n * FFZ // 2
    weight = pl.BlockSpec((part, n, FFZ), lambda i, c: (i, 0, 0))
    outs = [pl.BlockSpec((part, w), lambda i, c: (i, 0)) for w in (span, 2 * span)]
    shapes = [jax.ShapeDtypeStruct((rows, w), BF) for w in (span, 2 * span)]
    return pl.pallas_call(
        prepare_body,
        grid_spec=pltpu.PrefetchScalarGridSpec(
            num_scalar_prefetch=1, grid=(rows // part,), in_specs=[weight] * 3, out_specs=outs * 2
        ),
        out_shape=shapes * 2,
        cost_estimate=lasts(5),
        compiler_params=pltpu.CompilerParams(vmem_limit_bytes=40 * MB),
    )(core, down, gate, up)


def finish_body(core_ref, *refs):
    n_own = (len(refs) - 5) // 2
    own_a, own_b = refs[:n_own], refs[n_own : 2 * n_own]
    got_a, got_b = refs[2 * n_own], refs[2 * n_own + 1]
    outs = refs[2 * n_own + 2 :]
    first = core_ref[0] == 0
    rows, n4, _ = outs[0].shape
    n = n4 // 4
    for m, out in enumerate(outs):
        flat = out.reshape(rows * n4, FFZ)
        for s, (own, got) in enumerate(((own_a, got_a), (own_b, got_b))):
            for e in range(n):
                cols = slice((m * n + e) * FFZ, (m * n + e + 1) * FFZ)
                mine = own[0][:, cols].astype(F32)
                for ref in own[1:]:
                    mine = mine + ref[:, cols].astype(F32)
                theirs = got[:, cols].astype(F32)
                flat[pl.ds(s * n + e, rows, stride=n4), :] = jnp.where(first, mine, theirs)
                flat[pl.ds(2 * n + s * n + e, rows, stride=n4), :] = jnp.where(first, theirs, mine)

def finish(core, own_a, own_b, got_a, got_b, experts):
    rows, wide = got_a.shape
    part = 48
    steps = rows // part
    own = pl.BlockSpec((part, wide), lambda i, c: (c[0] * steps + i, 0))
    got = pl.BlockSpec((part, wide), lambda i, c: (i, 0))
    out = pl.BlockSpec((part, experts, FFZ), lambda i, c: (i, 0, 0))
    return pl.pallas_call(
        finish_body,
        grid_spec=pltpu.PrefetchScalarGridSpec(num_scalar_prefetch=1, grid=(steps,),
            in_specs=[own] * (len(own_a) + len(own_b)) + [got] * 2, out_specs=[out] * 3),
        out_shape=[jax.ShapeDtypeStruct((rows, experts, FFZ), F32)] * 3,
        cost_estimate=lasts(9),
        compiler_params=pltpu.CompilerParams(vmem_limit_bytes=40 * MB),
    )(core, *own_a, *own_b, got_a, got_b)


def dot(a, b, dims=((1,), (0,)), out=F32):
    return lax.dot_general(a, b, (dims, ((), ())), preferred_element_type=F32).astype(out)


def flip(bit, size):
    return [(i, i ^ bit) for i in range(size)]


def swap_core(x):
    return lax.ppermute(x, "gx", flip(1, lax.axis_size("gx")))


def swap_x(x):
    return lax.ppermute(x, "gx", flip(2, lax.axis_size("gx")))


def swap_y(x):
    return lax.ppermute(x, "gx", flip(4, lax.axis_size("gx")))


def core_groups(size):
    return [[i for i in range(size) if i % 2 == c] for c in range(2)]


def after(x, *earlier):
    return lax.optimization_barrier((x, earlier))[0]


def plane_sum(x):
    size = lax.axis_size("gy")
    total = x
    for d in range(1, size):
        total = total + lax.ppermute(x, "gy", [(i, (i + d) % size) for i in range(size)])
    return total


def plane_shift(x, d):
    size = lax.axis_size("gy")
    return lax.ppermute(x, "gy", [(i, (i + d) % size) for i in range(size)])


def plane_pieces(x):
    return [x] + [plane_shift(x, d) for d in range(1, 4)]


def plane_scatter(parts):
    return lax.psum_scatter(parts, "gy", scatter_dimension=0, tiled=True)


def draw_body(c_ref, w_ref, o_ref):
    o_ref[...] = jnp.dot(c_ref[...], w_ref[...], preferred_element_type=F32).astype(BF)


def expert_draw(c, w_down):
    tokens = c.shape[0]
    width = w_down.shape[1]
    cols = 2 * FFZ
    return pl.pallas_call(
        draw_body,
        grid=(width // cols,),
        in_specs=[
            pl.BlockSpec((tokens, D), lambda j: (0, 0)),
            pl.BlockSpec((D, cols), lambda j: (0, j)),
        ],
        out_specs=pl.BlockSpec((tokens, cols), lambda j: (0, j)),
        out_shape=jax.ShapeDtypeStruct((tokens, width), BF),
        cost_estimate=lasts(22),
        compiler_params=pltpu.CompilerParams(vmem_limit_bytes=48 * MB),
    )(c, w_down)


def norm_pieces(slots_ref, pieces, gains, normed_ref, scale_ref, joined_ref):
    cols = pieces[0].shape[1]
    total = 0.0
    for ref in pieces:
        x = ref[...].astype(F32)
        total = total + jnp.sum(x * x, axis=1, keepdims=True)
    scale = lax.rsqrt(total / D + epsilon)
    scale_ref[...] = scale
    for d, ref in enumerate(pieces):
        at = pl.ds(pl.multiple_of(slots_ref[d] * cols, 128), cols)
        x = ref[...]
        if joined_ref is not None:
            joined_ref[:, at] = x
        normed_ref[:, at] = (x.astype(F32) * scale * gains[d].astype(F32)).astype(BF)


def first_norm_body(slots_ref, *refs):
    pieces, tails, (normed_ref, scale_ref, gain_ref) = refs[:4], refs[4:8], refs[8:]
    cols = pieces[0].shape[1]
    norm_pieces(slots_ref, pieces, [ref[0:1] for ref in tails], normed_ref, scale_ref, None)
    for d, ref in enumerate(tails):
        gain_ref[:, pl.ds(pl.multiple_of(slots_ref[d] * cols, 128), cols)] = ref[...]


def second_norm_body(slots_ref, *refs):
    pieces, gain_ref, (normed_ref, scale_ref, joined_ref) = refs[:4], refs[4], refs[5:]
    cols = pieces[0].shape[1]
    gains = [gain_ref[1:2, pl.ds(pl.multiple_of(slots_ref[d] * cols, 128), cols)] for d in range(4)]
    norm_pieces(slots_ref, pieces, gains, normed_ref, scale_ref, joined_ref)


def norm_planes(slots, pieces, gains=None):
    first = gains is None
    cols = pieces[0].shape[1]
    length = pieces[0].shape[0] - (16 if first else 0)
    rows = 256
    wide = pl.BlockSpec((rows, D), lambda i, s: (i, 0))
    piece = pl.BlockSpec((rows, cols), lambda i, s: (i, 0))
    tail = pl.BlockSpec((16, cols), lambda i, s: (length // 16, 0))
    all_gains = pl.BlockSpec((16, D), lambda i, s: (0, 0))
    shape = jax.ShapeDtypeStruct
    return pl.pallas_call(
        first_norm_body if first else second_norm_body,
        grid_spec=pltpu.PrefetchScalarGridSpec(
            num_scalar_prefetch=1,
            grid=(length // rows,),
            in_specs=[piece] * 4 + ([tail] * 4 if first else [all_gains]),
            out_specs=[wide, pl.BlockSpec((rows, 1), lambda i, s: (i, 0)), all_gains if first else wide],
        ),
        out_shape=[
            shape((length, D), BF),
            shape((length, 1), F32),
            shape((16, D) if first else (length, D), BF),
        ],
        cost_estimate=lasts(6),
    )(slots, *pieces, *(pieces if first else [gains]))


def lay_body(slots_ref, *refs):
    cols = refs[0].shape[1]
    for d in range(4):
        refs[4][:, pl.ds(pl.multiple_of(slots_ref[d] * cols, 128), cols)] = refs[d][...]


def lay_planes(slots, pieces):
    rows, cols = pieces[0].shape
    return pl.pallas_call(
        lay_body,
        in_specs=[pl.BlockSpec(memory_space=pltpu.SMEM)] + [VM] * 4,
        out_specs=VM,
        out_shape=jax.ShapeDtypeStruct((rows, D), pieces[0].dtype),
        cost_estimate=lasts(3),
    )(slots, *pieces)


def spread_body(slots_ref, a_ref, w_ref, *outs):
    a = a_ref[...]
    cols = outs[0].shape[1]
    for d, o_ref in enumerate(outs):
        w = w_ref[pl.ds(pl.multiple_of(slots_ref[d] * cols, 128), cols), :]
        o_ref[...] = lax.dot_general(a, w, (((1,), (1,)), ((), ())), preferred_element_type=F32).astype(BF)


def spread(slots, a, w):
    rows = a.shape[0]
    return pl.pallas_call(
        spread_body,
        in_specs=[pl.BlockSpec(memory_space=pltpu.SMEM), VM, VM],
        out_specs=[VM] * 4,
        out_shape=[jax.ShapeDtypeStruct((rows, D // 4), BF)] * 4,
        cost_estimate=lasts(5),
    )(slots, a, w)


def pad_lanes(x, width=128):
    return jnp.pad(x, ((0, 0), (0, width - x.shape[1])))


def shards(
    tokens,
    first_gain,
    w_query,
    w_key,
    w_value,
    w_out,
    second_gain,
    w_router,
    w_gate,
    w_up,
    w_down,
    routes,
    block_cotangent,
):
    length, slice_cols = tokens.shape
    rows_here = w_query.shape[0]
    chip_rows = 2 * rows_here
    heads = w_query.shape[1] // HD
    groups = w_key.shape[1] // HD
    experts_n = w_router.shape[1]
    mine_n = experts_n // 2
    span = mine_n * w_gate.shape[2]
    planes = lax.axis_size("gy")
    size = lax.axis_size("gx")
    core = lax.axis_index("gx") % 2
    chip = lax.axis_index("gx") // 2
    core_array = core.astype(jnp.int32)[None]
    plane = lax.axis_index("gy")
    small_mesh = size == 8

    def core_order(own, other):
        return jnp.where(core == 0, own, other), jnp.where(core == 0, other, own)

    before = jnp.stack([(plane - d) % planes for d in range(4)]).astype(jnp.int32)
    onward = jnp.stack([(plane + d) % planes for d in range(4)]).astype(jnp.int32)

    gain_rows = jnp.pad(jnp.stack([first_gain, second_gain]).astype(BF), ((0, 14), (0, 0)))
    joined = lax.all_gather(jnp.concatenate([tokens, gain_rows], axis=0), "gy", axis=1, tiled=True)
    gains = joined[length:]
    gain_two = gains[1:2].astype(F32)

    attn_own = jnp.concatenate(
        [w_query.astype(BF), w_key.astype(BF), w_value.astype(BF), w_out.astype(BF), pad_lanes(w_router.astype(BF))],
        axis=1,
    )
    if small_mesh:
        attn_pair = jnp.concatenate(core_order(attn_own, swap_core(attn_own)), axis=0)
        half = attn_pair.shape[1] // 2
        attn_x, attn_y = swap_x(attn_pair), swap_y(attn_pair)
        attn_corner = jnp.concatenate([swap_y(attn_x[:, :half]), swap_x(attn_y[:, half:])], axis=1)
        attn_whole = jnp.zeros((4 * chip_rows, 2 * half), BF)
        for k, piece in enumerate((attn_pair, attn_x, attn_y, attn_corner)):
            attn_whole = lax.dynamic_update_slice(attn_whole, piece, ((chip ^ k) * chip_rows, 0))
    else:
        attn_whole = lax.all_gather(attn_own, "gx", axis=0, tiled=True)
    keep_d, keep_gu, give_d, give_gu = prepare(core_array, w_down, w_gate, w_up)
    pair_d = jnp.concatenate(core_order(keep_d, swap_core(give_d)), axis=0)
    pair_gu = jnp.concatenate(core_order(keep_gu, swap_core(give_gu)), axis=0)
    w_down_all = lax.all_gather(pair_d, "gx", axis=0, tiled=True, axis_index_groups=core_groups(size))
    w_gu_all = lax.all_gather(pair_gu, "gx", axis=0, tiled=True, axis_index_groups=core_groups(size))
    query_cols, pair_cols = w_query.shape[1], w_key.shape[1]
    qkv_cols = query_cols + 2 * pair_cols
    qkv_w = attn_whole[:, :qkv_cols]
    out_w = attn_whole[:, qkv_cols : qkv_cols + w_out.shape[1]]
    router_w = attn_whole[:, qkv_cols + w_out.shape[1] :]

    xf = joined[:length].astype(F32)
    scale_one = lax.rsqrt(jnp.mean(xf * xf, axis=1, keepdims=True) + epsilon)
    normed_one = (xf * scale_one * gains[0:1].astype(F32)).astype(BF)
    cot_pieces = plane_pieces(after(block_cotangent, normed_one))
    qkv_raw = dot(after(normed_one, pair_d, pair_gu), qkv_w)
    mixed, q_rot, k_rot, v_rot, log_total = attend(qkv_raw, heads, groups)
    attn_parts = spread(onward, mixed, out_w)
    token_slice = tokens.astype(F32)
    residual = token_slice + attn_parts[0].astype(F32)
    for d in range(1, 4):
        residual = residual + plane_shift(attn_parts[d], d).astype(F32)
    res_pieces = plane_pieces(residual.astype(BF))

    cot_own = lay_planes(before, after(tuple(cot_pieces), *attn_parts))
    cot_both = jnp.concatenate([cot_own, swap_core(cot_own)], axis=0)
    down_raw = expert_draw(cot_both, w_down_all)

    iota = lax.broadcasted_iota(jnp.int32, (2 * length, 128), 1)
    routes_both = jnp.concatenate([routes, swap_core(routes)], axis=0)
    member = routes_both[:, 0:1] == iota
    for k in range(1, routes.shape[1]):
        member = member | (routes_both[:, k : k + 1] == iota)

    normed_own, scale_own, residual_own = norm_planes(before, after(tuple(res_pieces), down_raw), gains)
    normed_two = jnp.concatenate([normed_own, swap_core(normed_own)], axis=0)

    logits = jnp.where(member, dot(normed_two, router_w), masked)
    gate_exp = jnp.exp(logits - jnp.max(logits, axis=1, keepdims=True))
    gate_all = gate_exp / jnp.sum(gate_exp, axis=1, keepdims=True)
    gate_mine = pad_lanes(lax.dynamic_slice_in_dim(gate_all, core * mine_n, mine_n, 1))
    grads, dsum = expert_forward(normed_two, w_gu_all, down_raw, gate_mine, 2 * length, 256)

    def back_half(i, grads):
        block = (1, length, span)
        return project([(grads, block, (1, i, 0), w_gu_all, 0), (grads, block, (2, i, 0), w_gu_all, 1)], planes)

    dsum_planes = plane_sum(dsum[:, :mine_n].T)
    back_other = back_half(1, grads)
    back_own = back_half(0, after(grads, back_other))
    back_other = swap_core(back_other)
    back_own = after(back_own, dsum_planes)
    back_sum = (back_own.astype(F32) + back_other.astype(F32)).astype(BF)
    back_slice = plane_scatter(back_sum).astype(F32)

    if small_mesh:
        def terms(a, b, inputs):
            ids = jnp.stack([chip ^ k for k in a + b]).astype(jnp.int32)
            return expert_terms(ids, *inputs, chip_rows)

        inputs = after((cot_both, normed_two, grads), back_own)
        give_a, give_b = terms((1, 3), (2, 3), inputs)
        got_a, got_b = swap_x(give_a), swap_y(give_b)
        own_a, own_b = terms((0, 2), (0, 1), after(inputs, give_a, give_b))
        moe_inputs = after((grads, w_down_all), own_a, own_b)
        next_a = (own_a[chip_rows:].astype(F32) + got_a[chip_rows:].astype(F32)).astype(BF)
        next_b = (own_b[chip_rows:].astype(F32) + got_b[chip_rows:].astype(F32)).astype(BF)
        last_a, last_b = swap_y(next_a), swap_x(next_b)
        sum_a, sum_b = [own_a, got_a, last_a], [own_b, got_b, last_b]
    else:
        moe_inputs = (grads, w_down_all)
        next_a = next_b = back_sum

        def whole_term(side, m):
            left = cot_both if m == 0 else normed_two
            right = grads[m][:, side * (span // 2) : (side + 1) * (span // 2)]
            return dot(left, right, ((0,), (0,)), BF)

        def chips_sum(side):
            whole = jnp.concatenate([whole_term(side, m) for m in range(3)], axis=1)
            return [
                lax.psum_scatter(
                    whole, "gx", scatter_dimension=0, tiled=True, axis_index_groups=core_groups(size)
                )
            ]

        sum_a, sum_b = chips_sum(0), chips_sum(1)

    dsum_got = swap_core(dsum_planes[:, length:])
    dsum_all = jnp.concatenate(core_order(dsum_planes[:, :length], dsum_got), axis=0).T
    gate_own = gate_all[:length, :experts_n]
    grad_picked = gate_own * (dsum_all - jnp.sum(gate_own * dsum_all, axis=1, keepdims=True))
    grad_logits = grad_picked.astype(BF)
    router_slice = lax.dynamic_slice_in_dim(router_w[:, :experts_n], plane * slice_cols, slice_cols, 0)
    grad_normed_two = back_slice + dot(grad_logits, router_slice, ((1,), (1,)))
    grad_h2_full = lax.all_gather(grad_normed_two.astype(BF), "gy", axis=1, tiled=True)

    def partner_rows(parts):
        picked = [lax.dynamic_slice_in_dim(p, (1 - core) * rows_here, rows_here, 0).astype(F32) for p in parts]
        return swap_core(sum(picked).astype(BF))


    def moe_half(i):
        return project([(moe_inputs[0], (1, length, span), (0, i, 0), moe_inputs[1], 0)], planes)

    moe_other = swap_core(moe_half(1))
    moe_parts = (moe_half(0).astype(F32) + moe_other.astype(F32)).astype(BF)
    moe_slice = plane_scatter(after(moe_parts, grad_h2_full))
    block_out = (residual + moe_slice.astype(F32)).astype(BF)

    grad_h2_full = after(grad_h2_full, moe_parts)
    residual_f = residual_own.astype(F32)
    grad_h2_f = grad_h2_full.astype(F32)
    inner = jnp.sum(grad_h2_f * gain_two * residual_f, axis=1, keepdims=True)
    grad_res_full = (
        cot_own.astype(F32)
        + scale_own * grad_h2_f * gain_two
        - residual_f * scale_own * scale_own * scale_own * inner / D
    ).astype(BF)
    gain_two_slice = second_gain.astype(BF).astype(F32)
    grad_residual = (
        block_cotangent.astype(F32)
        + scale_own * grad_normed_two * gain_two_slice
        - residual * scale_own * scale_own * scale_own * inner / D
    )
    second_gain_grad = jnp.sum(grad_normed_two * residual * scale_own, axis=0)

    grad_mixed = dot(grad_res_full, out_w, out=BF)
    grad_qkv = after(attend_back(q_rot, k_rot, v_rot, log_total, mixed, grad_mixed), next_a, next_b)
    dh_parts = project([(grad_qkv, (length, qkv_cols), (0, 0), qkv_w, 0)], planes)
    grad_normed_one = plane_scatter(after(dh_parts, moe_slice)).astype(F32)
    sum_a, sum_b = after((sum_a, sum_b), dh_parts)
    down_grad, gate_grad, up_grad = finish(
        core_array, sum_a, sum_b, partner_rows(sum_a), partner_rows(sum_b), experts_n
    )

    left = after((grad_res_full, normed_one), dh_parts)
    attn_terms = jnp.concatenate(
        [dot(left[1], grad_qkv, ((0,), (0,)), BF), dot(left[0], mixed, ((0,), (0,)), BF),
         pad_lanes(dot(normed_two[:length], grad_logits, ((0,), (0,)), BF))],
        axis=1,
    )
    attn_sums = chips_total(attn_terms, chip, core, rows_here)
    query_grad = attn_sums[:, :query_cols]
    key_grad = attn_sums[:, query_cols : query_cols + pair_cols]
    value_grad = attn_sums[:, query_cols + pair_cols : qkv_cols]
    out_grad = attn_sums[:, qkv_cols : qkv_cols + w_out.shape[1]]
    router_grad = attn_sums[:, qkv_cols + w_out.shape[1] :][:, :experts_n]

    gain_one_slice = first_gain.astype(BF).astype(F32)
    scaled = grad_normed_one * gain_one_slice
    inner_one = jnp.sum(grad_qkv.astype(F32) * qkv_raw, axis=1)[None, :]
    inner_one = plane_sum(after(inner_one, grad_normed_one))[0][:, None]
    first_gain_grad = jnp.sum(grad_normed_one * token_slice * scale_one, axis=0)
    first_gain_grad, second_gain_grad = lax.psum((first_gain_grad, second_gain_grad), "gx")
    input_grad = (
        grad_residual
        + scale_one * scaled
        - token_slice * scale_one * scale_one * inner_one / D
    ).astype(BF)
    return (
        block_out,
        input_grad,
        first_gain_grad,
        query_grad,
        key_grad,
        value_grad,
        out_grad,
        second_gain_grad,
        router_grad,
        gate_grad,
        up_grad,
        down_grad,
    )


def chips_total(terms, chip, core, rows_here):
    size = lax.axis_size("gx")
    if size != 8:
        return lax.psum_scatter(terms, "gx", scatter_dimension=0, tiled=True).astype(F32)
    cols = terms.shape[1]
    blocks = terms.reshape(4, 2, rows_here, cols)
    keep = jnp.where(core == 0, blocks[:, 0], blocks[:, 1])
    give = jnp.where(core == 0, blocks[:, 1], blocks[:, 0])
    mine = (keep.astype(F32) + swap_core(give).astype(F32)).astype(BF)
    half = cols // 2

    def part(k, side):
        return lax.dynamic_index_in_dim(mine, chip ^ k, 0, False)[:, side * half : (side + 1) * half]

    give_a = jnp.stack([part(1, 0), part(3, 0)])
    give_b = jnp.stack([part(2, 1), part(3, 1)])
    got_a, got_b = swap_x(give_a).astype(F32), swap_y(give_b).astype(F32)
    last_a = swap_y((part(2, 0).astype(F32) + got_a[1]).astype(BF))
    last_b = swap_x((part(1, 1).astype(F32) + got_b[1]).astype(BF))
    return jnp.concatenate(
        [part(0, 0).astype(F32) + got_a[0] + last_a.astype(F32), part(0, 1).astype(F32) + got_b[0] + last_b.astype(F32)],
        axis=1,
    )


def solution(mesh):
    placed = (
        P("gx", "gy"),
        P("gy"),
        P("gx", "gy"),
        P("gx", "gy"),
        P("gx", "gy"),
        P("gx", "gy"),
        P("gy"),
        P("gx", None),
        P("gx", None, "gy"),
        P("gx", None, "gy"),
        P("gx", None, "gy"),
        P("gx", None),
        P("gx", "gy"),
    )
    return jax.shard_map(
        shards,
        mesh=mesh,
        in_specs=placed,
        out_specs=(
            P("gx", "gy"),
            P("gx", "gy"),
            P("gy"),
            P("gx", "gy"),
            P("gx", "gy"),
            P("gx", "gy"),
            P("gx", "gy"),
            P("gy"),
            P("gx", None),
            P("gx", None, "gy"),
            P("gx", None, "gy"),
            P("gx", None, "gy"),
        ),
        check_vma=False,
    )
```

```python
from functools import partial
import math

import jax
import jax.numpy as jnp
import numpy as np
from jax import lax
from jax.experimental import pallas as pl
from jax.experimental.pallas import tpu as pltpu
from jax.sharding import PartitionSpec as P

D = 1536
HD = 64
FFZ = 128
epsilon = 1e-06
BF = jnp.bfloat16
F32 = jnp.float32
masked = -1e30
VM = pl.BlockSpec(memory_space=pltpu.VMEM)
MB = 1024 * 1024


def lasts(us):
    return pl.CostEstimate(flops=int(us * 0.45e9), bytes_accessed=int(us * 1.1e6), transcendentals=0)


def rope_tables(length):
    frequency = np.exp(np.arange(HD // 2) * (-2.0 * math.log(10000.0) / HD)).astype(np.float32)
    angles = np.arange(length, dtype=np.float32)[:, None] * frequency[None, :]
    cosine, sine_tab = np.cos(angles), np.sin(angles)
    return (
        jnp.asarray(np.concatenate([cosine, cosine], axis=1), F32),
        jnp.asarray(np.concatenate([-sine_tab, sine_tab], axis=1), F32),
    )

def halves_swapped(x):
    return jnp.concatenate([x[:, HD // 2 :], x[:, : HD // 2]], axis=1)

def causal_scores(q, keys, first):
    rows, length = q.shape[0], keys.shape[0]
    scores = lax.dot_general(q, keys, (((1,), (1,)), ((), ())), preferred_element_type=F32)
    row_ids = first + lax.broadcasted_iota(jnp.int32, (rows, length), 0)
    col_ids = lax.broadcasted_iota(jnp.int32, (rows, length), 1)
    return jnp.where(col_ids <= row_ids, scores, masked)

def attend_body(heads, groups, block, qkv_ref, cos_ref, sin_ref, mixed_ref, q_ref, k_ref, v_ref, log_ref, mixed_scr):
    length = qkv_ref.shape[0]
    cosine, sine = cos_ref[...], sin_ref[...]
    for h in range(heads + groups):
        x = qkv_ref[:, h * HD : (h + 1) * HD]
        x = (x * cosine + halves_swapped(x) * sine).astype(BF)
        if h < heads:
            q_ref[h] = x * jnp.asarray(HD**-0.5, BF)
        else:
            k_ref[h - heads] = x
    for g in range(groups):
        at = (heads + groups + g) * HD
        v_ref[g] = qkv_ref[:, at : at + HD].astype(BF)
    log_ref[...] = jnp.zeros_like(log_ref)
    share = heads // groups

    def head(h, carry):
        group = h // share
        for i in range(length // block):
            rows = slice(i * block, (i + 1) * block)
            seen = slice(0, (i + 1) * block)
            scores = causal_scores(q_ref[h, rows], k_ref[group, seen], i * block)
            top = jnp.max(scores, axis=1, keepdims=True)
            expo = jnp.exp(scores - top)
            total = jnp.sum(expo, axis=1, keepdims=True)
            probs = (expo * (1.0 / total)).astype(BF)
            mixed_scr[h, rows] = jnp.dot(probs, v_ref[group, seen], preferred_element_type=F32).astype(BF)
            lanes = lax.broadcasted_iota(jnp.int32, (block, 128), 1)
            log_ref[rows] = jnp.where(lanes == h, top + jnp.log(total), log_ref[rows])
        return carry

    lax.fori_loop(0, heads, head, 0)
    for h in range(0, heads, 2):
        mixed_ref[:, h * HD : (h + 2) * HD] = jnp.concatenate([mixed_scr[h], mixed_scr[h + 1]], axis=1)

def attend(qkv, heads, groups, block=256):
    length = qkv.shape[0]
    cosine, sine = rope_tables(length)
    S = jax.ShapeDtypeStruct
    return pl.pallas_call(
        partial(attend_body, heads, groups, block),
        in_specs=[VM] * 3,
        out_specs=[VM] * 5,
        out_shape=[
            S((length, heads * HD), BF),
            S((heads, length, HD), BF),
            S((groups, length, HD), BF),
            S((groups, length, HD), BF),
            S((length, 128), F32),
        ],
        scratch_shapes=[pltpu.VMEM((heads, length, HD), BF)],
        cost_estimate=lasts(17),
        compiler_params=pltpu.CompilerParams(vmem_limit_bytes=40 * MB),
    )(qkv, cosine, sine)

def attend_back_body(heads, groups, block, q_ref, k_ref, v_ref, log_ref, mixed_ref, do_ref, cos_ref, sin_ref, out_ref, do_scr, mixed_scr, dq_scr, dk_scr, dv_scr):
    length = do_ref.shape[0]
    share = heads // groups
    for h in range(heads):
        do_scr[h] = do_ref[:, h * HD : (h + 1) * HD]
        mixed_scr[h] = mixed_ref[:, h * HD : (h + 1) * HD]
    dk_scr[...] = jnp.zeros_like(dk_scr)
    dv_scr[...] = jnp.zeros_like(dv_scr)

    def head(h, carry):
        group = h // share
        for i in range(length // block):
            rows = slice(i * block, (i + 1) * block)
            seen = slice(0, (i + 1) * block)
            q, keys, values, do = q_ref[h, rows], k_ref[group, seen], v_ref[group, seen], do_scr[h, rows]
            lanes = lax.broadcasted_iota(jnp.int32, (block, 128), 1)
            log_total = jnp.sum(jnp.where(lanes == h, log_ref[rows], 0.0), axis=1, keepdims=True)
            probs = jnp.exp(causal_scores(q, keys, i * block) - log_total)
            grad_probs = lax.dot_general(do, values, (((1,), (1,)), ((), ())), preferred_element_type=F32)
            inner = jnp.sum(do.astype(F32) * mixed_scr[h, rows].astype(F32), axis=1, keepdims=True)
            grad_scores = (probs * (grad_probs - inner)).astype(BF)
            dq_scr[h, rows] = jnp.dot(grad_scores, keys, preferred_element_type=F32) * (HD**-0.5)
            across = (((0,), (0,)), ((), ()))
            dk_scr[group, seen] += lax.dot_general(grad_scores, q, across, preferred_element_type=F32)
            dv_scr[group, seen] += lax.dot_general(probs.astype(BF), do, across, preferred_element_type=F32)
        return carry

    lax.fori_loop(0, heads, head, 0)
    cosine, sine = cos_ref[...], sin_ref[...]

    def back(x):
        return (x * cosine - halves_swapped(x) * sine).astype(BF)

    cols = [back(dq_scr[h]) for h in range(heads)]
    cols += [back(dk_scr[g]) for g in range(groups)]
    cols += [dv_scr[g].astype(BF) for g in range(groups)]
    for p in range(0, len(cols), 2):
        out_ref[:, p * HD : (p + 2) * HD] = jnp.concatenate([cols[p], cols[p + 1]], axis=1)

def attend_back(q, k, v, log_total, mixed, do, block=256):
    heads, length, _ = q.shape
    groups = k.shape[0]
    cosine, sine = rope_tables(length)
    return pl.pallas_call(
        partial(attend_back_body, heads, groups, block),
        in_specs=[VM] * 8,
        out_specs=VM,
        out_shape=jax.ShapeDtypeStruct((length, (heads + 2 * groups) * HD), BF),
        scratch_shapes=[
            pltpu.VMEM((heads, length, HD), BF),
            pltpu.VMEM((heads, length, HD), BF),
            pltpu.VMEM((heads, length, HD), F32),
            pltpu.VMEM((groups, length, HD), F32),
            pltpu.VMEM((groups, length, HD), F32),
        ],
        cost_estimate=lasts(19),
        compiler_params=pltpu.CompilerParams(vmem_limit_bytes=48 * MB),
    )(q, k, v, log_total, mixed, do, cosine, sine)

def expert_math(gate, draw, gg, uu):
    sig = 1.0 / (1.0 + jnp.exp(-gg))
    silu = gg * sig
    act = silu * uu
    back = gate * draw
    return (
        (gate * act).astype(BF),
        (back * uu * (sig + silu * (1.0 - sig))).astype(BF),
        (back * silu).astype(BF),
        jnp.sum(act * draw, axis=1, keepdims=True),
    )

def expert_body(rows, chunk, h_ref, wg_ref, wu_ref, draw_ref, gate_ref, out_ref, dsum_ref):
    step = pl.program_id(1)
    wg, wu = wg_ref[...], wu_ref[...]
    for m in range(rows // chunk):
        at = slice(m * chunk, (m + 1) * chunk)
        h = h_ref[at]
        g = jnp.dot(h, wg, preferred_element_type=F32)
        u = jnp.dot(h, wu, preferred_element_type=F32)
        lanes = lax.broadcasted_iota(jnp.int32, (chunk, 128), 1)
        gates = gate_ref[at]
        sums = jnp.where(step == 0, 0.0, dsum_ref[at])
        for half in range(2):
            cols = slice(half * FFZ, (half + 1) * FFZ)
            hot = lanes == step * 2 + half
            gate = jnp.sum(jnp.where(hot, gates, 0.0), axis=1, keepdims=True)
            ga, dg, du, s = expert_math(gate, draw_ref[at, cols].astype(F32), g[:, cols], u[:, cols])
            out_ref[0, at, cols] = ga
            out_ref[1, at, cols] = dg
            out_ref[2, at, cols] = du
            sums = jnp.where(hot, s, sums)
        dsum_ref[at] = sums

def expert_forward(h, w_gu, draw, gate, rows=1024, chunk=256):
    tokens, width = draw.shape
    steps = width // (2 * FFZ)
    return pl.pallas_call(
        partial(expert_body, rows, chunk),
        grid=(tokens // rows, steps),
        in_specs=[
            pl.BlockSpec((rows, D), lambda i, j: (i, 0)),
            pl.BlockSpec((D, 2 * FFZ), lambda i, j: (0, j)),
            pl.BlockSpec((D, 2 * FFZ), lambda i, j: (0, steps + j)),
            pl.BlockSpec((rows, 2 * FFZ), lambda i, j: (i, j)),
            pl.BlockSpec((rows, 128), lambda i, j: (i, 0)),
        ],
        out_specs=[
            pl.BlockSpec((3, rows, 2 * FFZ), lambda i, j: (0, i, j)),
            pl.BlockSpec((rows, 128), lambda i, j: (i, 0)),
        ],
        out_shape=[
            jax.ShapeDtypeStruct((3, tokens, width), BF),
            jax.ShapeDtypeStruct((tokens, 128), F32),
        ],
        cost_estimate=lasts(46),
        compiler_params=pltpu.CompilerParams(vmem_limit_bytes=56 * MB),
    )(h, w_gu, w_gu, draw, gate)

def project_body(n, *refs):
    dims = (((1,), (1,)), ((), ()))
    o_ref = refs[2 * n]
    total = None
    for a_ref, w_ref in zip(refs[:n], refs[n : 2 * n]):
        a = a_ref[0] if len(a_ref.shape) == 3 else a_ref[...]
        term = lax.dot_general(a, w_ref[...], dims, preferred_element_type=F32)
        total = term if total is None else total + term
    cols = o_ref.shape[2]
    o_ref[0] = total[:, :cols].astype(BF)
    o_ref[1] = total[:, cols:].astype(BF)

def project(terms, parts):
    rows, width = terms[0][1][-2:]
    cols = D // parts
    n = len(terms)
    total = pl.pallas_call(
        partial(project_body, n),
        grid=(parts // 2,),
        in_specs=[pl.BlockSpec(t[1], partial(lambda at, j: at, t[2])) for t in terms]
        + [pl.BlockSpec((2 * cols, width), partial(lambda at, j: (j, at), t[4])) for t in terms],
        out_specs=pl.BlockSpec((2, rows, cols), lambda j: (j, 0, 0)),
        out_shape=jax.ShapeDtypeStruct((parts, rows, cols), BF),
        cost_estimate=lasts(rows * width * D * n / 3.5e8 + 2),
        compiler_params=pltpu.CompilerParams(vmem_limit_bytes=56 * MB),
    )(*[t[0] for t in terms], *[t[3] for t in terms])
    return total.reshape(parts * rows, cols)

def term_body(steps, ids_ref, c0_ref, c1_ref, h0_ref, h1_ref, g_ref, a_ref, b_ref):
    side, m = pl.program_id(0), pl.program_id(1)
    rows = c0_ref.shape[1]
    across = (((0,), (0,)), ((), ()))

    def work(l0, l1, o_ref):
        g = g_ref[0]
        o_ref[:rows] = lax.dot_general(l0[...], g, across, preferred_element_type=F32).astype(BF)
        o_ref[rows:] = lax.dot_general(l1[...], g, across, preferred_element_type=F32).astype(BF)

    for s, o_ref in ((0, a_ref), (1, b_ref)):
        @pl.when((side == s) & (m == 0))
        def _():
            work(c0_ref, c1_ref, o_ref)

        @pl.when((side == s) & (m > 0))
        def _():
            work(h0_ref, h1_ref, o_ref)

def expert_terms(ids, c, h, grads, rows, cols=1280):
    tokens, width = grads.shape[1:]
    steps = width // 2 // cols
    last = 3 * steps - 1
    piece = lambda p: pl.BlockSpec((tokens, rows), lambda s, m, j, ids: (0, ids[2 * s + p]))
    out = jax.ShapeDtypeStruct((2 * rows, 3 * width // 2), BF)
    return pl.pallas_call(
        partial(term_body, steps),
        grid_spec=pltpu.PrefetchScalarGridSpec(
            num_scalar_prefetch=1,
            grid=(2, 3, steps),
            in_specs=[piece(0), piece(1), piece(0), piece(1),
                pl.BlockSpec((1, tokens, cols), lambda s, m, j, ids: (m, 0, s * steps + j))],
            out_specs=[
                pl.BlockSpec((2 * rows, cols), lambda s, m, j, ids: (0, jnp.where(s == 0, m * steps + j, last))),
                pl.BlockSpec((2 * rows, cols), lambda s, m, j, ids: (0, jnp.where(s == 0, 0, m * steps + j))),
            ],
        ),
        out_shape=[out, out],
        cost_estimate=lasts(34),
        compiler_params=pltpu.CompilerParams(vmem_limit_bytes=56 * MB),
    )(ids, c, c, h, h, grads)

def prepare_body(core_ref, down_ref, gate_ref, up_ref, keep_d_ref, keep_gu_ref, give_d_ref, give_gu_ref):
    first = core_ref[0] == 0
    rows, n2, _ = down_ref.shape
    n = n2 // 2
    for m, ref in enumerate((down_ref, gate_ref, up_ref)):
        flat = ref.reshape(rows * n2, FFZ)
        keep_ref, give_ref = (keep_d_ref, give_d_ref) if m == 0 else (keep_gu_ref, give_gu_ref)
        for e in range(n):
            lo = flat[pl.ds(e, rows, stride=n2), :]
            hi = flat[pl.ds(n + e, rows, stride=n2), :]
            at = (max(m - 1, 0) * n + e) * FFZ
            keep_ref[:, at : at + FFZ] = jnp.where(first, lo, hi).astype(BF)
            give_ref[:, at : at + FFZ] = jnp.where(first, hi, lo).astype(BF)


def prepare(core, down, gate, up):
    rows, n, _ = down.shape
    part = 48
    span = n * FFZ // 2
    weight = pl.BlockSpec((part, n, FFZ), lambda i, c: (i, 0, 0))
    outs = [pl.BlockSpec((part, w), lambda i, c: (i, 0)) for w in (span, 2 * span)]
    shapes = [jax.ShapeDtypeStruct((rows, w), BF) for w in (span, 2 * span)]
    return pl.pallas_call(
        prepare_body,
        grid_spec=pltpu.PrefetchScalarGridSpec(
            num_scalar_prefetch=1, grid=(rows // part,), in_specs=[weight] * 3, out_specs=outs * 2
        ),
        out_shape=shapes * 2,
        cost_estimate=lasts(5),
        compiler_params=pltpu.CompilerParams(vmem_limit_bytes=40 * MB),
    )(core, down, gate, up)


def finish_body(core_ref, *refs):
    n_own = (len(refs) - 5) // 2
    own_a, own_b = refs[:n_own], refs[n_own : 2 * n_own]
    got_a, got_b = refs[2 * n_own], refs[2 * n_own + 1]
    outs = refs[2 * n_own + 2 :]
    first = core_ref[0] == 0
    rows, n4, _ = outs[0].shape
    n = n4 // 4
    for m, out in enumerate(outs):
        flat = out.reshape(rows * n4, FFZ)
        for s, (own, got) in enumerate(((own_a, got_a), (own_b, got_b))):
            for e in range(n):
                cols = slice((m * n + e) * FFZ, (m * n + e + 1) * FFZ)
                mine = own[0][:, cols].astype(F32)
                for ref in own[1:]:
                    mine = mine + ref[:, cols].astype(F32)
                theirs = got[:, cols].astype(F32)
                flat[pl.ds(s * n + e, rows, stride=n4), :] = jnp.where(first, mine, theirs)
                flat[pl.ds(2 * n + s * n + e, rows, stride=n4), :] = jnp.where(first, theirs, mine)

def finish(core, own_a, own_b, got_a, got_b, experts):
    rows, wide = got_a.shape
    part = 48
    steps = rows // part
    own = pl.BlockSpec((part, wide), lambda i, c: (c[0] * steps + i, 0))
    got = pl.BlockSpec((part, wide), lambda i, c: (i, 0))
    out = pl.BlockSpec((part, experts, FFZ), lambda i, c: (i, 0, 0))
    return pl.pallas_call(
        finish_body,
        grid_spec=pltpu.PrefetchScalarGridSpec(num_scalar_prefetch=1, grid=(steps,),
            in_specs=[own] * (len(own_a) + len(own_b)) + [got] * 2, out_specs=[out] * 3),
        out_shape=[jax.ShapeDtypeStruct((rows, experts, FFZ), F32)] * 3,
        cost_estimate=lasts(9),
        compiler_params=pltpu.CompilerParams(vmem_limit_bytes=40 * MB),
    )(core, *own_a, *own_b, got_a, got_b)


def dot(a, b, dims=((1,), (0,)), out=F32):
    return lax.dot_general(a, b, (dims, ((), ())), preferred_element_type=F32).astype(out)


def flip(bit, size):
    return [(i, i ^ bit) for i in range(size)]


def swap_core(x):
    return lax.ppermute(x, "gx", flip(1, lax.axis_size("gx")))


def swap_x(x):
    return lax.ppermute(x, "gx", flip(2, lax.axis_size("gx")))


def swap_y(x):
    return lax.ppermute(x, "gx", flip(4, lax.axis_size("gx")))


def core_groups(size):
    return [[i for i in range(size) if i % 2 == c] for c in range(2)]


def after(x, *earlier):
    return lax.optimization_barrier((x, earlier))[0]


def plane_sum(x):
    size = lax.axis_size("gy")
    total = x
    for d in range(1, size):
        total = total + lax.ppermute(x, "gy", [(i, (i + d) % size) for i in range(size)])
    return total


def plane_shift(x, d):
    size = lax.axis_size("gy")
    return lax.ppermute(x, "gy", [(i, (i + d) % size) for i in range(size)])


def plane_pieces(x):
    return [x] + [plane_shift(x, d) for d in range(1, 4)]


def plane_scatter(parts):
    return lax.psum_scatter(parts, "gy", scatter_dimension=0, tiled=True)


def draw_body(c_ref, w_ref, o_ref):
    o_ref[...] = jnp.dot(c_ref[...], w_ref[...], preferred_element_type=F32).astype(BF)


def expert_draw(c, w_down):
    tokens = c.shape[0]
    width = w_down.shape[1]
    cols = 2 * FFZ
    return pl.pallas_call(
        draw_body,
        grid=(width // cols,),
        in_specs=[
            pl.BlockSpec((tokens, D), lambda j: (0, 0)),
            pl.BlockSpec((D, cols), lambda j: (0, j)),
        ],
        out_specs=pl.BlockSpec((tokens, cols), lambda j: (0, j)),
        out_shape=jax.ShapeDtypeStruct((tokens, width), BF),
        cost_estimate=lasts(22),
        compiler_params=pltpu.CompilerParams(vmem_limit_bytes=48 * MB),
    )(c, w_down)


def norm_pieces(slots_ref, pieces, gains, normed_ref, scale_ref, joined_ref):
    cols = pieces[0].shape[1]
    total = 0.0
    for ref in pieces:
        x = ref[...].astype(F32)
        total = total + jnp.sum(x * x, axis=1, keepdims=True)
    scale = lax.rsqrt(total / D + epsilon)
    scale_ref[...] = scale
    for d, ref in enumerate(pieces):
        at = pl.ds(pl.multiple_of(slots_ref[d] * cols, 128), cols)
        x = ref[...]
        if joined_ref is not None:
            joined_ref[:, at] = x
        normed_ref[:, at] = (x.astype(F32) * scale * gains[d].astype(F32)).astype(BF)


def first_norm_body(slots_ref, *refs):
    pieces, tails, (normed_ref, scale_ref, gain_ref) = refs[:4], refs[4:8], refs[8:]
    cols = pieces[0].shape[1]
    norm_pieces(slots_ref, pieces, [ref[0:1] for ref in tails], normed_ref, scale_ref, None)
    for d, ref in enumerate(tails):
        gain_ref[:, pl.ds(pl.multiple_of(slots_ref[d] * cols, 128), cols)] = ref[...]


def second_norm_body(slots_ref, *refs):
    pieces, gain_ref, (normed_ref, scale_ref, joined_ref) = refs[:4], refs[4], refs[5:]
    cols = pieces[0].shape[1]
    gains = [gain_ref[1:2, pl.ds(pl.multiple_of(slots_ref[d] * cols, 128), cols)] for d in range(4)]
    norm_pieces(slots_ref, pieces, gains, normed_ref, scale_ref, joined_ref)


def norm_planes(slots, pieces, gains=None):
    first = gains is None
    cols = pieces[0].shape[1]
    length = pieces[0].shape[0] - (16 if first else 0)
    rows = 256
    wide = pl.BlockSpec((rows, D), lambda i, s: (i, 0))
    piece = pl.BlockSpec((rows, cols), lambda i, s: (i, 0))
    tail = pl.BlockSpec((16, cols), lambda i, s: (length // 16, 0))
    all_gains = pl.BlockSpec((16, D), lambda i, s: (0, 0))
    shape = jax.ShapeDtypeStruct
    return pl.pallas_call(
        first_norm_body if first else second_norm_body,
        grid_spec=pltpu.PrefetchScalarGridSpec(
            num_scalar_prefetch=1,
            grid=(length // rows,),
            in_specs=[piece] * 4 + ([tail] * 4 if first else [all_gains]),
            out_specs=[wide, pl.BlockSpec((rows, 1), lambda i, s: (i, 0)), all_gains if first else wide],
        ),
        out_shape=[
            shape((length, D), BF),
            shape((length, 1), F32),
            shape((16, D) if first else (length, D), BF),
        ],
        cost_estimate=lasts(6),
    )(slots, *pieces, *(pieces if first else [gains]))


def lay_body(slots_ref, *refs):
    cols = refs[0].shape[1]
    for d in range(4):
        refs[4][:, pl.ds(pl.multiple_of(slots_ref[d] * cols, 128), cols)] = refs[d][...]


def lay_planes(slots, pieces):
    rows, cols = pieces[0].shape
    return pl.pallas_call(
        lay_body,
        in_specs=[pl.BlockSpec(memory_space=pltpu.SMEM)] + [VM] * 4,
        out_specs=VM,
        out_shape=jax.ShapeDtypeStruct((rows, D), pieces[0].dtype),
        cost_estimate=lasts(3),
    )(slots, *pieces)


def spread_body(slots_ref, a_ref, w_ref, *outs):
    a = a_ref[...]
    cols = outs[0].shape[1]
    for d, o_ref in enumerate(outs):
        w = w_ref[pl.ds(pl.multiple_of(slots_ref[d] * cols, 128), cols), :]
        o_ref[...] = lax.dot_general(a, w, (((1,), (1,)), ((), ())), preferred_element_type=F32).astype(BF)


def spread(slots, a, w):
    rows = a.shape[0]
    return pl.pallas_call(
        spread_body,
        in_specs=[pl.BlockSpec(memory_space=pltpu.SMEM), VM, VM],
        out_specs=[VM] * 4,
        out_shape=[jax.ShapeDtypeStruct((rows, D // 4), BF)] * 4,
        cost_estimate=lasts(5),
    )(slots, a, w)


def pad_lanes(x, width=128):
    return jnp.pad(x, ((0, 0), (0, width - x.shape[1])))


def shards(
    tokens,
    first_gain,
    w_query,
    w_key,
    w_value,
    w_out,
    second_gain,
    w_router,
    w_gate,
    w_up,
    w_down,
    routes,
    block_cotangent,
):
    length, slice_cols = tokens.shape
    rows_here = w_query.shape[0]
    chip_rows = 2 * rows_here
    heads = w_query.shape[1] // HD
    groups = w_key.shape[1] // HD
    experts_n = w_router.shape[1]
    mine_n = experts_n // 2
    span = mine_n * w_gate.shape[2]
    planes = lax.axis_size("gy")
    size = lax.axis_size("gx")
    core = lax.axis_index("gx") % 2
    chip = lax.axis_index("gx") // 2
    core_array = core.astype(jnp.int32)[None]
    plane = lax.axis_index("gy")
    small_mesh = size == 8

    def core_order(own, other):
        return jnp.where(core == 0, own, other), jnp.where(core == 0, other, own)

    before = jnp.stack([(plane - d) % planes for d in range(4)]).astype(jnp.int32)
    onward = jnp.stack([(plane + d) % planes for d in range(4)]).astype(jnp.int32)

    gain_rows = jnp.pad(jnp.stack([first_gain, second_gain]).astype(BF), ((0, 14), (0, 0)))
    joined = lax.all_gather(jnp.concatenate([tokens, gain_rows], axis=0), "gy", axis=1, tiled=True)
    gains = joined[length:]
    gain_two = gains[1:2].astype(F32)

    attn_own = jnp.concatenate(
        [w_query.astype(BF), w_key.astype(BF), w_value.astype(BF), w_out.astype(BF), pad_lanes(w_router.astype(BF))],
        axis=1,
    )
    if small_mesh:
        attn_pair = jnp.concatenate(core_order(attn_own, swap_core(attn_own)), axis=0)
        half = attn_pair.shape[1] // 2
        attn_x, attn_y = swap_x(attn_pair), swap_y(attn_pair)
        attn_corner = jnp.concatenate([swap_y(attn_x[:, :half]), swap_x(attn_y[:, half:])], axis=1)
        attn_whole = jnp.zeros((4 * chip_rows, 2 * half), BF)
        for k, piece in enumerate((attn_pair, attn_x, attn_y, attn_corner)):
            attn_whole = lax.dynamic_update_slice(attn_whole, piece, ((chip ^ k) * chip_rows, 0))
    else:
        attn_whole = lax.all_gather(attn_own, "gx", axis=0, tiled=True)
    keep_d, keep_gu, give_d, give_gu = prepare(core_array, w_down, w_gate, w_up)
    pair_d = jnp.concatenate(core_order(keep_d, swap_core(give_d)), axis=0)
    pair_gu = jnp.concatenate(core_order(keep_gu, swap_core(give_gu)), axis=0)
    w_down_all = lax.all_gather(pair_d, "gx", axis=0, tiled=True, axis_index_groups=core_groups(size))
    w_gu_all = lax.all_gather(pair_gu, "gx", axis=0, tiled=True, axis_index_groups=core_groups(size))
    query_cols, pair_cols = w_query.shape[1], w_key.shape[1]
    qkv_cols = query_cols + 2 * pair_cols
    qkv_w = attn_whole[:, :qkv_cols]
    out_w = attn_whole[:, qkv_cols : qkv_cols + w_out.shape[1]]
    router_w = attn_whole[:, qkv_cols + w_out.shape[1] :]

    xf = joined[:length].astype(F32)
    scale_one = lax.rsqrt(jnp.mean(xf * xf, axis=1, keepdims=True) + epsilon)
    normed_one = (xf * scale_one * gains[0:1].astype(F32)).astype(BF)
    cot_pieces = plane_pieces(after(block_cotangent, normed_one))
    qkv_raw = dot(after(normed_one, pair_d, pair_gu), qkv_w)
    mixed, q_rot, k_rot, v_rot, log_total = attend(qkv_raw, heads, groups)
    attn_parts = spread(onward, mixed, out_w)
    token_slice = tokens.astype(F32)
    residual = token_slice + attn_parts[0].astype(F32)
    for d in range(1, 4):
        residual = residual + plane_shift(attn_parts[d], d).astype(F32)
    res_pieces = plane_pieces(residual.astype(BF))

    cot_own = lay_planes(before, after(tuple(cot_pieces), *attn_parts))
    cot_both = jnp.concatenate([cot_own, swap_core(cot_own)], axis=0)
    down_raw = expert_draw(cot_both, w_down_all)

    iota = lax.broadcasted_iota(jnp.int32, (2 * length, 128), 1)
    routes_both = jnp.concatenate([routes, swap_core(routes)], axis=0)
    member = routes_both[:, 0:1] == iota
    for k in range(1, routes.shape[1]):
        member = member | (routes_both[:, k : k + 1] == iota)

    normed_own, scale_own, residual_own = norm_planes(before, after(tuple(res_pieces), down_raw, routes_both), gains)
    normed_two = jnp.concatenate([normed_own, swap_core(normed_own)], axis=0)

    logits = jnp.where(member, dot(normed_two, router_w), masked)
    gate_exp = jnp.exp(logits - jnp.max(logits, axis=1, keepdims=True))
    gate_all = gate_exp / jnp.sum(gate_exp, axis=1, keepdims=True)
    gate_mine = pad_lanes(lax.dynamic_slice_in_dim(gate_all, core * mine_n, mine_n, 1))
    grads, dsum = expert_forward(normed_two, w_gu_all, down_raw, gate_mine, 2 * length, 256)

    def back_half(i, grads):
        block = (1, length, span)
        return project([(grads, block, (1, i, 0), w_gu_all, 0), (grads, block, (2, i, 0), w_gu_all, 1)], planes)

    dsum_planes = plane_sum(dsum[:, :mine_n].T)
    back_other = back_half(1, grads)
    back_own = back_half(0, after(grads, back_other))
    back_other = swap_core(back_other)
    back_own = after(back_own, dsum_planes)
    back_sum = (back_own.astype(F32) + back_other.astype(F32)).astype(BF)
    back_slice = plane_scatter(back_sum).astype(F32)

    if small_mesh:
        def terms(a, b, inputs):
            ids = jnp.stack([chip ^ k for k in a + b]).astype(jnp.int32)
            return expert_terms(ids, *inputs, chip_rows)

        inputs = after((cot_both, normed_two, grads), back_own)
        give_a, give_b = terms((1, 3), (2, 3), inputs)
        got_a, got_b = swap_x(give_a), swap_y(give_b)
        own_a, own_b = terms((0, 2), (0, 1), after(inputs, give_a, give_b))
        moe_inputs = after((grads, w_down_all), own_a, own_b)
        next_a = (own_a[chip_rows:].astype(F32) + got_a[chip_rows:].astype(F32)).astype(BF)
        next_b = (own_b[chip_rows:].astype(F32) + got_b[chip_rows:].astype(F32)).astype(BF)
        last_a, last_b = swap_y(next_a), swap_x(next_b)
        sum_a, sum_b = [own_a, got_a, last_a], [own_b, got_b, last_b]
    else:
        moe_inputs = (grads, w_down_all)
        next_a = next_b = back_sum

        def whole_term(side, m):
            left = cot_both if m == 0 else normed_two
            right = grads[m][:, side * (span // 2) : (side + 1) * (span // 2)]
            return dot(left, right, ((0,), (0,)), BF)

        def chips_sum(side):
            whole = jnp.concatenate([whole_term(side, m) for m in range(3)], axis=1)
            return [
                lax.psum_scatter(
                    whole, "gx", scatter_dimension=0, tiled=True, axis_index_groups=core_groups(size)
                )
            ]

        sum_a, sum_b = chips_sum(0), chips_sum(1)

    dsum_got = swap_core(dsum_planes[:, length:])
    dsum_all = jnp.concatenate(core_order(dsum_planes[:, :length], dsum_got), axis=0).T
    gate_own = gate_all[:length, :experts_n]
    grad_picked = gate_own * (dsum_all - jnp.sum(gate_own * dsum_all, axis=1, keepdims=True))
    grad_logits = grad_picked.astype(BF)
    router_slice = lax.dynamic_slice_in_dim(router_w[:, :experts_n], plane * slice_cols, slice_cols, 0)
    grad_normed_two = back_slice + dot(grad_logits, router_slice, ((1,), (1,)))
    grad_h2_full = lax.all_gather(grad_normed_two.astype(BF), "gy", axis=1, tiled=True)

    def partner_rows(parts):
        picked = [lax.dynamic_slice_in_dim(p, (1 - core) * rows_here, rows_here, 0).astype(F32) for p in parts]
        return swap_core(sum(picked).astype(BF))


    def moe_half(i):
        return project([(moe_inputs[0], (1, length, span), (0, i, 0), moe_inputs[1], 0)], planes)

    moe_other = swap_core(moe_half(1))
    moe_parts = (moe_half(0).astype(F32) + moe_other.astype(F32)).astype(BF)
    moe_slice = plane_scatter(after(moe_parts, grad_h2_full))
    block_out = (residual + moe_slice.astype(F32)).astype(BF)

    grad_h2_full = after(grad_h2_full, moe_parts)
    residual_f = residual_own.astype(F32)
    grad_h2_f = grad_h2_full.astype(F32)
    inner = jnp.sum(grad_h2_f * gain_two * residual_f, axis=1, keepdims=True)
    grad_res_full = (
        cot_own.astype(F32)
        + scale_own * grad_h2_f * gain_two
        - residual_f * scale_own * scale_own * scale_own * inner / D
    ).astype(BF)
    gain_two_slice = second_gain.astype(BF).astype(F32)
    grad_residual = (
        block_cotangent.astype(F32)
        + scale_own * grad_normed_two * gain_two_slice
        - residual * scale_own * scale_own * scale_own * inner / D
    )
    second_gain_grad = jnp.sum(grad_normed_two * residual * scale_own, axis=0)

    grad_mixed = dot(grad_res_full, out_w, out=BF)
    grad_qkv = after(attend_back(q_rot, k_rot, v_rot, log_total, mixed, grad_mixed), next_a, next_b)
    dh_parts = project([(grad_qkv, (length, qkv_cols), (0, 0), qkv_w, 0)], planes)
    grad_normed_one = plane_scatter(after(dh_parts, moe_slice)).astype(F32)
    sum_a, sum_b = after((sum_a, sum_b), dh_parts)
    down_grad, gate_grad, up_grad = finish(
        core_array, sum_a, sum_b, partner_rows(sum_a), partner_rows(sum_b), experts_n
    )

    left = after((grad_res_full, normed_one), dh_parts)
    attn_terms = jnp.concatenate(
        [dot(left[1], grad_qkv, ((0,), (0,)), BF), dot(left[0], mixed, ((0,), (0,)), BF),
         pad_lanes(dot(normed_two[:length], grad_logits, ((0,), (0,)), BF))],
        axis=1,
    )
    attn_sums = chips_total(attn_terms, chip, core, rows_here)
    query_grad = attn_sums[:, :query_cols]
    key_grad = attn_sums[:, query_cols : query_cols + pair_cols]
    value_grad = attn_sums[:, query_cols + pair_cols : qkv_cols]
    out_grad = attn_sums[:, qkv_cols : qkv_cols + w_out.shape[1]]
    router_grad = attn_sums[:, qkv_cols + w_out.shape[1] :][:, :experts_n]

    gain_one_slice = first_gain.astype(BF).astype(F32)
    scaled = grad_normed_one * gain_one_slice
    inner_one = jnp.sum(grad_qkv.astype(F32) * qkv_raw, axis=1)[None, :]
    inner_one = plane_sum(after(inner_one, grad_normed_one))[0][:, None]
    first_gain_grad = jnp.sum(grad_normed_one * token_slice * scale_one, axis=0)
    first_gain_grad, second_gain_grad = lax.psum((first_gain_grad, second_gain_grad), "gx")
    input_grad = (
        grad_residual
        + scale_one * scaled
        - token_slice * scale_one * scale_one * inner_one / D
    ).astype(BF)
    return (
        block_out,
        input_grad,
        first_gain_grad,
        query_grad,
        key_grad,
        value_grad,
        out_grad,
        second_gain_grad,
        router_grad,
        gate_grad,
        up_grad,
        down_grad,
    )


def chips_total(terms, chip, core, rows_here):
    size = lax.axis_size("gx")
    if size != 8:
        return lax.psum_scatter(terms, "gx", scatter_dimension=0, tiled=True).astype(F32)
    cols = terms.shape[1]
    blocks = terms.reshape(4, 2, rows_here, cols)
    keep = jnp.where(core == 0, blocks[:, 0], blocks[:, 1])
    give = jnp.where(core == 0, blocks[:, 1], blocks[:, 0])
    mine = (keep.astype(F32) + swap_core(give).astype(F32)).astype(BF)
    half = cols // 2

    def part(k, side):
        return lax.dynamic_index_in_dim(mine, chip ^ k, 0, False)[:, side * half : (side + 1) * half]

    give_a = jnp.stack([part(1, 0), part(3, 0)])
    give_b = jnp.stack([part(2, 1), part(3, 1)])
    got_a, got_b = swap_x(give_a).astype(F32), swap_y(give_b).astype(F32)
    last_a = swap_y((part(2, 0).astype(F32) + got_a[1]).astype(BF))
    last_b = swap_x((part(1, 1).astype(F32) + got_b[1]).astype(BF))
    return jnp.concatenate(
        [part(0, 0).astype(F32) + got_a[0] + last_a.astype(F32), part(0, 1).astype(F32) + got_b[0] + last_b.astype(F32)],
        axis=1,
    )


def solution(mesh):
    placed = (
        P("gx", "gy"),
        P("gy"),
        P("gx", "gy"),
        P("gx", "gy"),
        P("gx", "gy"),
        P("gx", "gy"),
        P("gy"),
        P("gx", None),
        P("gx", None, "gy"),
        P("gx", None, "gy"),
        P("gx", None, "gy"),
        P("gx", None),
        P("gx", "gy"),
    )
    return jax.shard_map(
        shards,
        mesh=mesh,
        in_specs=placed,
        out_specs=(
            P("gx", "gy"),
            P("gx", "gy"),
            P("gy"),
            P("gx", "gy"),
            P("gx", "gy"),
            P("gx", "gy"),
            P("gx", "gy"),
            P("gy"),
            P("gx", None),
            P("gx", None, "gy"),
            P("gx", None, "gy"),
            P("gx", None, "gy"),
        ),
        check_vma=False,
    )
```
